32 devices in a mesh: row: 8 (over y, x, core), col: 4 (over z).
Axes of the slice: x: 2, y: 2, z: 4, core: 2. Of those that a mesh axis runs over, the one named last changes fastest.
Arguments:
- features: bfloat16 [4096, 256], P(('row', 'col')), may hold values from -6 to 6
- tile_values: bfloat16 [8, 4, 8, 128, 128], P('row', 'col'), may hold values from -0.21875 to 0.21875
- tile_rows: int32 [8, 4, 8], P('row', 'col'), may hold values from 0 to 3, as said below
- tile_cols: int32 [8, 4, 8], P('row', 'col'), may hold values from 0 to 7
- tile_count: int32 [8, 4], P('row', 'col'), may hold values from 1 to 8, as said below
- weight: bfloat16 [256, 256], replicated, may hold values from -0.375 to 0.375
- out_grad: bfloat16 [4096, 256], P(('row', 'col')), may hold values from -6 to 6
Outputs:
- activated: bfloat16 [4096, 256], P(('row', 'col'))
- feature_grad: bfloat16 [4096, 256], P(('row', 'col'))
- weight_grad: float32 [256, 256], replicated
The draws below stay inside these ranges and needn't reach their ends.
Inputs may be any that keep to these rules, and one draw needn't show every extreme that they name: Within one grid cell the pairs (tile_rows, tile_cols) of all 8 slots are distinct. `tile_count`: some grid cell has all 8 slots live.
All inputs are finite; a program needn't handle non-finite values.
Results may differ from the reference program's by a relative error of at most 0.023.
Values may be sent and summed in bfloat16 or wider, within the bound.
A program may use at most 64 MiB of HBM per device.

```python
import jax
import jax.numpy as jnp
from jax import lax

F = 256
TILE = 128
SB = 128
NODES = 4096
ROW_TILES = 4
COL_TILES = 8
TILES_MAX = 8
N_ROW = 8
N_COL = 4


def tile_layout(key):
    base = jax.random.fold_in(key, 7)
    cell_keys = jax.random.split(base, N_ROW * N_COL)
    orders = jax.vmap(lambda cell_key: jax.random.permutation(cell_key, ROW_TILES * COL_TILES))(cell_keys)
    return orders[:, :TILES_MAX].astype(jnp.int32).reshape(N_ROW, N_COL, TILES_MAX)


def draw_tile_rows(key, part):
    return tile_layout(key) // COL_TILES


def draw_tile_cols(key, part):
    return tile_layout(key) % COL_TILES


def draw_tile_count(key, part):
    lowest = max(1, TILES_MAX // 2)
    counts = jax.random.randint(jax.random.fold_in(key, 11), (N_ROW * N_COL,), lowest, TILES_MAX + 1, dtype=jnp.int32)
    busiest = jax.random.randint(jax.random.fold_in(key, 12), (), 0, N_ROW * N_COL, dtype=jnp.int32)
    counts = counts.at[busiest].set(TILES_MAX)
    return counts.reshape(N_ROW, N_COL)


def levels(key, shape, shards, least, top_value):
    def one(dim, shards_of):
        steps = jax.random.uniform(jax.random.fold_in(jax.random.fold_in(key, 6), dim), (shards_of,), jnp.float32, least / len(shards), top_value / len(shards))
        return jnp.repeat(jnp.exp(steps), shape[dim] // shards_of).reshape((-1,) + (1,) * (len(shape) - dim - 1))

    level = one(*shards[0])
    for cut in shards[1:]:
        level = level * one(*cut)
    return level


def centred(key, dims, width, limit, cuts=(), held_as=jnp.bfloat16):
    entries = width * jax.random.normal(key, dims, jnp.float32)
    if cuts:
        entries = entries * levels(key, dims, cuts, -0.22, 0.18)
    return jnp.clip(entries, -limit, limit).astype(held_as)


def setup_inputs(seed: int = 0) -> dict:
    splits = jax.random.split(jax.random.key(seed), 8)
    features = centred(splits[0], (NODES, F), 1.0, 6.0, ((0, 32),))
    tile_values = centred(splits[1], (N_ROW, N_COL, TILES_MAX, TILE, TILE), (max(TILE, 3 * TILES_MAX * TILE * TILE // (4 * SB))) ** -0.5, 0.21875, ((0, 8), (1, 4)))
    tile_rows = draw_tile_rows(jax.random.fold_in(splits[7], 71), 0)
    tile_cols = draw_tile_cols(jax.random.fold_in(splits[7], 71), 0)
    tile_count = draw_tile_count(jax.random.fold_in(splits[7], 71), 0)
    weight = centred(splits[5], (F, F), F ** -0.5, 0.375)
    out_grad = centred(splits[6], (NODES, F), 1.0, 6.0, ((0, 32),))
    return dict(features=features, tile_values=tile_values, tile_rows=tile_rows, tile_cols=tile_cols, tile_count=tile_count, weight=weight, out_grad=out_grad)


def gelu_value(preact):
    return jax.nn.gelu(preact, approximate=True)

def gelu_backward(preact, upstream):
    _, pullback = jax.vjp(gelu_value, preact)
    return pullback(upstream)[0]

def reference(features, tile_values, tile_rows, tile_cols, tile_count, weight, out_grad):
    block_rows = N_COL * SB
    block_cols = N_ROW * SB
    projected = jnp.dot(features, weight, preferred_element_type=jnp.float32).astype(jnp.bfloat16)
    projected_cells = projected.reshape(N_ROW, N_COL, SB, F)

    def forward_row(row_index):

        def grid_cell(col_index, summed):
            source = projected_cells[:, col_index].reshape(block_cols, F)

            def tile_step(slot, running):
                row_tile = tile_rows[row_index, col_index, slot]
                col_tile = tile_cols[row_index, col_index, slot]
                picked = lax.dynamic_slice_in_dim(source, col_tile * TILE, TILE, 0)
                products = jnp.dot(tile_values[row_index, col_index, slot], picked, preferred_element_type=jnp.float32)
                current = lax.dynamic_slice_in_dim(running, row_tile * TILE, TILE, 0)
                return lax.dynamic_update_slice_in_dim(running, current + products, row_tile * TILE, 0)
            running = lax.fori_loop(jnp.int32(0), tile_count[row_index, col_index], tile_step, jnp.zeros((block_rows, F), jnp.float32))
            rounded = lax.optimization_barrier(running.astype(jnp.bfloat16)).astype(jnp.float32)
            return summed + rounded
        return lax.fori_loop(jnp.int32(0), jnp.int32(N_COL), grid_cell, jnp.zeros((block_rows, F), jnp.float32))
    preact = lax.map(forward_row, jnp.arange(N_ROW, dtype=jnp.int32)).reshape(NODES, F)
    activated = gelu_value(preact).astype(jnp.bfloat16)
    cotangent = gelu_backward(preact, out_grad.astype(jnp.float32)).astype(jnp.bfloat16)
    cotangent_rows = cotangent.reshape(N_ROW, block_rows, F)

    def backward_col(col_index):

        def grid_cell(row_index, summed):
            source = cotangent_rows[row_index]

            def tile_step(slot, running):
                row_tile = tile_rows[row_index, col_index, slot]
                col_tile = tile_cols[row_index, col_index, slot]
                picked = lax.dynamic_slice_in_dim(source, row_tile * TILE, TILE, 0)
                products = jnp.dot(tile_values[row_index, col_index, slot].T, picked, preferred_element_type=jnp.float32)
                current = lax.dynamic_slice_in_dim(running, col_tile * TILE, TILE, 0)
                return lax.dynamic_update_slice_in_dim(running, current + products, col_tile * TILE, 0)
            running = lax.fori_loop(jnp.int32(0), tile_count[row_index, col_index], tile_step, jnp.zeros((block_cols, F), jnp.float32))
            rounded = lax.optimization_barrier(running.astype(jnp.bfloat16)).astype(jnp.float32)
            return summed + rounded
        return lax.fori_loop(jnp.int32(0), jnp.int32(N_ROW), grid_cell, jnp.zeros((block_cols, F), jnp.float32))
    pulled_cols = lax.map(backward_col, jnp.arange(N_COL, dtype=jnp.int32))
    pulled = pulled_cols.reshape(N_COL, N_ROW, SB, F).transpose(1, 0, 2, 3).reshape(NODES, F).astype(jnp.bfloat16)
    weight_grad = jnp.dot(features.T, pulled, preferred_element_type=jnp.float32) * NODES ** (-0.5)
    feature_grad = jnp.dot(pulled, weight.T, preferred_element_type=jnp.float32).astype(jnp.bfloat16)
    return (activated, feature_grad, weight_grad)
```

```python
import functools

import jax
import jax.numpy as jnp
from jax import lax
from jax.experimental import pallas as pl
from jax.experimental.pallas import tpu as pltpu
from jax.sharding import PartitionSpec as P

MESH = pl.DeviceIdType.MESH
F32 = jnp.float32
BF16 = jnp.bfloat16


def repeat(low, high, step):
    if high - low <= 8:
        for k in range(low, high):
            step(k)
    else:

        def once(k, carry):
            step(k)
            return carry

        lax.fori_loop(low, high, once, 0)


def block(index, size):
    if isinstance(index, int):
        return pl.ds(index * size, size)
    return pl.ds(pl.multiple_of(index * size, size), size)


def dot(a, b):
    return jnp.dot(a, b, preferred_element_type=F32)


def gelu_and_slope(v):
    scale = 0.7978845608028654
    square = v * v
    t = jnp.tanh(scale * (v + 0.044715 * v * square))
    half = 0.5 * (1.0 + t)
    slope = half + 0.5 * v * (1.0 - t * t) * scale * (1.0 + 3 * 0.044715 * square)
    return v * half, slope


def kernel(
    n_row, n_col,
    feat_in, tiles_in, rows_ref, cols_ref, count_ref, weight_in, upstream_in,
    act_out, fgrad_out, wgrad_out,
    feat_all, tiles, tiles_t, adj, adj_t, weight, weight_t, upstream,
    part_send, part_recv, cot_all, back_send, back_recv,
    w_send, w_recv, w_mid, w_all, act, fgrad, wgrad,
    in_sem, out_sem,
    feat_s, feat_r, part_s, part_r, cot_s, cot_r, back_s, back_r,
    w1_s, w1_r, w2_s, w2_r, w3_s, w3_r,
):
    i, j = lax.axis_index("row"), lax.axis_index("col")
    nodes, width = feat_in.shape
    slots, tile = tiles_in.shape[0], tiles_in.shape[1]
    row_tiles = n_col * nodes // tile
    col_tiles = n_row * nodes // tile
    half = width // 2
    piece = 2 * width // n_row

    def row_peer(k):
        return lax.rem(i + k, n_row)

    def col_peer(k):
        return lax.rem(j + k, n_col)

    def to_row(src, dst, send, recv, peer):
        return pltpu.make_async_remote_copy(
            src_ref=src, dst_ref=dst, send_sem=send, recv_sem=recv,
            device_id=(peer, j), device_id_type=MESH)

    def to_col(src, dst, send, recv, peer):
        return pltpu.make_async_remote_copy(
            src_ref=src, dst_ref=dst, send_sem=send, recv_sem=recv,
            device_id=(i, peer), device_id_type=MESH)

    loads = [
        pltpu.make_async_copy(feat_in, feat_all.at[block(i, nodes)], in_sem.at[0]),
        pltpu.make_async_copy(tiles_in, tiles.at[pl.ds(0, slots)], in_sem.at[1]),
        pltpu.make_async_copy(weight_in, weight, in_sem.at[2]),
        pltpu.make_async_copy(upstream_in, upstream, in_sem.at[3]),
    ]
    for load in loads:
        load.start()

    barrier = pltpu.get_barrier_semaphore()
    repeat(1, n_row, lambda k: pl.semaphore_signal(
        barrier, inc=1, device_id=(row_peer(k), j), device_id_type=MESH))
    repeat(1, n_col, lambda k: pl.semaphore_signal(
        barrier, inc=1, device_id=(i, col_peer(k)), device_id_type=MESH))
    pl.semaphore_wait(barrier, n_row + n_col - 2)

    def feat_copy(k, owner, peer):
        return to_row(feat_in, feat_all.at[block(owner, nodes)],
                      feat_s.at[k], feat_r.at[k], peer)

    repeat(1, n_row, lambda k: feat_copy(k, i, row_peer(k)).start())

    loads[1].wait()
    tiles[slots] = jnp.zeros((tile, tile), BF16)
    tiles_t[slots] = jnp.zeros((tile, tile), BF16)

    def flip(s):
        tiles_t[s] = tiles[s].T

    repeat(0, slots, flip)
    count = count_ref[0, 0]

    def place_row(r):
        def place(c):
            slot = jnp.int32(slots)
            for s in range(slots):
                hit = (rows_ref[0, 0, s] == r) & (cols_ref[0, 0, s] == c) & (s < count)
                slot = jnp.where(hit, jnp.int32(s), slot)
            adj[block(r, tile), block(c, tile)] = tiles[slot]
            adj_t[block(c, tile), block(r, tile)] = tiles_t[slot]

        repeat(0, col_tiles, place)

    repeat(0, row_tiles, place_row)
    loads[2].wait()
    loads[3].wait()
    weight_t[...] = weight[...].T

    loads[0].wait()
    repeat(1, n_row, lambda k: feat_copy(k, row_peer(n_row - k), row_peer(k)).wait_recv())

    def part_copy(k, owner, peer):
        return to_col(part_send.at[peer], part_recv.at[owner],
                      part_s.at[k], part_r.at[k], peer)

    def forward(k):
        peer = col_peer(k)
        part_send[peer] = dot(adj[block(peer, nodes), :], feat_all[...]).astype(BF16)
        part_copy(k, j, peer).start()

    repeat(1, n_col, forward)
    part_recv[j] = dot(adj[block(j, nodes), :], feat_all[...]).astype(BF16)
    repeat(1, n_col, lambda k: part_copy(k, col_peer(n_col - k), col_peer(k)).wait_recv())
    total = part_recv[0].astype(F32)
    for k in range(1, n_col):
        total = total + part_recv[k].astype(F32)
    aggregate = total.astype(BF16)
    value, slope = gelu_and_slope(dot(aggregate, weight[...]))
    cotangent = (upstream[...].astype(F32) * slope).astype(BF16)

    cot_all[block(j, nodes), :] = cotangent

    def cot_copy(k, owner, peer):
        return to_col(cot_all.at[block(owner, nodes)], cot_all.at[block(owner, nodes)],
                      cot_s.at[k], cot_r.at[k], peer)

    repeat(1, n_col, lambda k: cot_copy(k, j, col_peer(k)).start())
    act[...] = value.astype(BF16)
    act_store = pltpu.make_async_copy(act, act_out, out_sem.at[0])
    act_store.start()

    term = lax.dot_general(aggregate, cotangent, (((0,), (0,)), ((), ())),
                           preferred_element_type=F32)
    term = (term * (nodes * n_row * n_col) ** -0.5).astype(BF16)
    w_send[pl.ds(0, width), :] = term[:, :half]
    w_send[pl.ds(width, width), :] = term[:, half:]

    def w1_copy(k, owner, peer):
        return to_row(w_send.at[block(peer, piece)], w_recv.at[owner],
                      w1_s.at[k], w1_r.at[k], peer)

    repeat(1, n_row, lambda k: w1_copy(k, i, row_peer(k)).start())
    w_recv[i] = w_send[block(i, piece), :]

    repeat(1, n_col, lambda k: cot_copy(k, col_peer(n_col - k), col_peer(k)).wait_recv())

    def back_copy(k, owner, peer):
        return to_row(back_send.at[peer], back_recv.at[owner],
                      back_s.at[k], back_r.at[k], peer)

    def backward(k):
        peer = row_peer(k)
        back_send[peer] = dot(adj_t[block(peer, nodes), :], cot_all[...]).astype(BF16)
        back_copy(k, i, peer).start()

    repeat(1, n_row, backward)
    back_recv[i] = dot(adj_t[block(i, nodes), :], cot_all[...]).astype(BF16)

    repeat(1, n_row, lambda k: w1_copy(k, row_peer(n_row - k), row_peer(k)).wait_recv())
    summed = w_recv[0].astype(F32)
    for k in range(1, n_row):
        summed = summed + w_recv[k].astype(F32)
    w_mid[j] = summed.astype(BF16)

    def w2_copy(k, owner, peer):
        return to_col(w_mid.at[owner], w_mid.at[owner], w2_s.at[k], w2_r.at[k], peer)

    repeat(1, n_col, lambda k: w2_copy(k, j, col_peer(k)).start())
    repeat(1, n_col, lambda k: w2_copy(k, col_peer(n_col - k), col_peer(k)).wait_recv())
    summed = w_mid[0].astype(F32)
    for k in range(1, n_col):
        summed = summed + w_mid[k].astype(F32)
    w_all[block(i, piece), :] = summed.astype(BF16)

    def w3_copy(k, owner, peer):
        return to_row(w_all.at[block(owner, piece)], w_all.at[block(owner, piece)],
                      w3_s.at[k], w3_r.at[k], peer)

    repeat(1, n_row, lambda k: w3_copy(k, i, row_peer(k)).start())

    repeat(1, n_row, lambda k: back_copy(k, row_peer(n_row - k), row_peer(k)).wait_recv())
    pulled = back_recv[0].astype(F32)
    for k in range(1, n_row):
        pulled = pulled + back_recv[k].astype(F32)
    fgrad[...] = dot(pulled.astype(BF16), weight_t[...]).astype(BF16)
    fgrad_store = pltpu.make_async_copy(fgrad, fgrad_out, out_sem.at[1])
    fgrad_store.start()

    repeat(1, n_row, lambda k: w3_copy(k, row_peer(n_row - k), row_peer(k)).wait_recv())
    wgrad[:, pl.ds(0, half)] = w_all[pl.ds(0, width), :].astype(F32)
    wgrad[:, pl.ds(half, half)] = w_all[pl.ds(width, width), :].astype(F32)
    wgrad_store = pltpu.make_async_copy(wgrad, wgrad_out, out_sem.at[2])
    wgrad_store.start()

    def row_sent(k):
        peer = row_peer(k)
        feat_copy(k, i, peer).wait_send()
        w1_copy(k, i, peer).wait_send()
        back_copy(k, i, peer).wait_send()
        w3_copy(k, i, peer).wait_send()

    def col_sent(k):
        peer = col_peer(k)
        part_copy(k, j, peer).wait_send()
        cot_copy(k, j, peer).wait_send()
        w2_copy(k, j, peer).wait_send()

    repeat(1, n_row, row_sent)
    repeat(1, n_col, col_sent)
    act_store.wait()
    fgrad_store.wait()
    wgrad_store.wait()


def body(features, tile_values, tile_rows, tile_cols, tile_count, weight, out_grad):
    n_row, n_col = lax.axis_size("row"), lax.axis_size("col")
    nodes, width = features.shape
    slots, tile = tile_values.shape[2], tile_values.shape[3]
    tall, wide = n_col * nodes, n_row * nodes
    piece = 2 * width // n_row
    vmem, dma = pltpu.VMEM, pltpu.SemaphoreType.DMA
    anywhere = pl.BlockSpec(memory_space=pl.ANY)
    scalars = pl.BlockSpec(memory_space=pltpu.SMEM)
    return tuple(pl.pallas_call(
        functools.partial(kernel, n_row, n_col),
        out_shape=(
            jax.ShapeDtypeStruct((nodes, width), BF16),
            jax.ShapeDtypeStruct((nodes, width), BF16),
            jax.ShapeDtypeStruct((width, width), F32),
        ),
        in_specs=[anywhere, anywhere, scalars, scalars, scalars, anywhere, anywhere],
        out_specs=(anywhere, anywhere, anywhere),
        scratch_shapes=[
            vmem((wide, width), BF16),
            vmem((slots + 1, tile, tile), BF16),
            vmem((slots + 1, tile, tile), BF16),
            vmem((tall, wide), BF16),
            vmem((wide, tall), BF16),
            vmem((width, width), BF16),
            vmem((width, width), BF16),
            vmem((nodes, width), BF16),
            vmem((n_col, nodes, width), BF16),
            vmem((n_col, nodes, width), BF16),
            vmem((tall, width), BF16),
            vmem((n_row, nodes, width), BF16),
            vmem((n_row, nodes, width), BF16),
            vmem((2 * width, width // 2), BF16),
            vmem((n_row, piece, width // 2), BF16),
            vmem((n_col, piece, width // 2), BF16),
            vmem((2 * width, width // 2), BF16),
            vmem((nodes, width), BF16),
            vmem((nodes, width), BF16),
            vmem((width, width), F32),
            dma((4,)), dma((3,)),
            dma((n_row,)), dma((n_row,)), dma((n_col,)), dma((n_col,)),
            dma((n_col,)), dma((n_col,)), dma((n_row,)), dma((n_row,)),
            dma((n_row,)), dma((n_row,)), dma((n_col,)), dma((n_col,)),
            dma((n_row,)), dma((n_row,)),
        ],
        compiler_params=pltpu.CompilerParams(
            collective_id=0, has_side_effects=True, vmem_limit_bytes=56 * 1024 * 1024),
    )(features, tile_values[0, 0], tile_rows, tile_cols, tile_count, weight, out_grad))


def solution(mesh):
    placed = (
        P(("row", "col"), None),
        P("row", "col", None, None, None),
        P("row", "col", None),
        P("row", "col", None),
        P("row", "col"),
        P(),
        P(("row", "col"), None),
    )
    return jax.shard_map(
        body,
        mesh=mesh,
        in_specs=placed,
        out_specs=(P(("row", "col"), None), P(("row", "col"), None), P()),
        check_vma=False,
    )
```

```python
import functools

import jax
import jax.numpy as jnp
from jax import lax
from jax.experimental import pallas as pl
from jax.experimental.pallas import tpu as pltpu
from jax.sharding import PartitionSpec as P

MESH = pl.DeviceIdType.MESH
F32 = jnp.float32
BF16 = jnp.bfloat16


def repeat(low, high, step):
    if high - low <= 8:
        for k in range(low, high):
            step(k)
    else:

        def once(k, carry):
            step(k)
            return carry

        lax.fori_loop(low, high, once, 0)


def block(index, size):
    if isinstance(index, int):
        return pl.ds(index * size, size)
    return pl.ds(pl.multiple_of(index * size, size), size)


def partner(rank, k, size):
    assert size & (size - 1) == 0
    found, bit = 0, 1
    while bit < size:
        found = found + bit * ((rank // bit + k // bit) % 2)
        bit *= 2
    return found


def far_first(size, step):
    repeat(1, size, lambda m: step(size - m))


def dot(a, b):
    return jnp.dot(a, b, preferred_element_type=F32)


def gelu_and_slope(v):
    scale = 0.7978845608028654
    square = v * v
    t = jnp.tanh(scale * (v + 0.044715 * v * square))
    half = 0.5 * (1.0 + t)
    slope = half + 0.5 * v * (1.0 - t * t) * scale * (1.0 + 3 * 0.044715 * square)
    return v * half, slope


PARTS = 1


def kernel(
    n_row, n_col,
    feat_in, tiles_in, rows_ref, cols_ref, count_ref, weight_in, upstream_in,
    act_out, fgrad_out, wgrad_out,
    feat_all, tiles, tiles_t, adj, adj_t, weight, weight_t, upstream,
    part_send, part_recv, cot_all, sib_send, sib_recv, back_send, back_recv,
    w_send, w_recv, w_mid, w_all, act, fgrad, wgrad,
    in_sem, out_sem, sib_s, sib_r,
    feat_s, feat_r, fwd_s, fwd_r, part_s, part_r, cot_s, cot_r,
    pair_s, pair_r, back_s, back_r, w1_s, w1_r, w2_s, w2_r, w3_s, w3_r,
):
    i, j = lax.axis_index("row"), lax.axis_index("col")
    chip, core = i // 2, i % 2
    n_chip = n_row // 2
    sibling = 2 * chip + 1 - core
    nodes, width = feat_in.shape
    slots, tile = tiles_in.shape[0], tiles_in.shape[1]
    row_tiles = n_col * nodes // tile
    col_tiles = n_row * nodes // tile
    half = width // 2
    piece = 2 * width // n_row
    lanes = width // PARTS

    def to_row(src, dst, send, recv, peer):
        return pltpu.make_async_remote_copy(
            src_ref=src, dst_ref=dst, send_sem=send, recv_sem=recv,
            device_id=(peer, j), device_id_type=MESH)

    def to_col(src, dst, send, recv, peer):
        return pltpu.make_async_remote_copy(
            src_ref=src, dst_ref=dst, send_sem=send, recv_sem=recv,
            device_id=(i, peer), device_id_type=MESH)

    def row_peer(k):
        return partner(i, k, n_row)

    def col_peer(k):
        return partner(j, k, n_col)

    def mate(k):
        return 2 * partner(chip, k, n_chip) + core

    def strip(h):
        return pl.ds(h * lanes, lanes)

    loads = [
        pltpu.make_async_copy(tiles_in, tiles.at[pl.ds(0, slots)], in_sem.at[0]),
        pltpu.make_async_copy(weight_in, weight, in_sem.at[1]),
        pltpu.make_async_copy(upstream_in, upstream, in_sem.at[2]),
    ] + [
        pltpu.make_async_copy(feat_in.at[:, strip(h)], feat_all.at[h, block(i, nodes)],
                              in_sem.at[3 + h])
        for h in range(PARTS)
    ]
    for load in loads:
        load.start()

    barrier = pltpu.get_barrier_semaphore()
    repeat(1, n_row, lambda k: pl.semaphore_signal(
        barrier, inc=1, device_id=(row_peer(k), j), device_id_type=MESH))
    repeat(1, n_col, lambda k: pl.semaphore_signal(
        barrier, inc=1, device_id=(i, col_peer(k)), device_id_type=MESH))
    pl.semaphore_wait(barrier, n_row + n_col - 2)

    def feat_copy(h, k, owner):
        return to_row(feat_in.at[:, strip(h)], feat_all.at[h, block(owner, nodes)],
                      feat_s.at[h, k], feat_r.at[h, k], mate(k))

    def sib_copy(h, owner):
        return to_row(feat_in.at[:, strip(h)], feat_all.at[h, block(owner, nodes)],
                      sib_s.at[h], sib_r.at[h], sibling)

    def pass_copy(h, k, owner):
        place = feat_all.at[h, block(owner, nodes)]
        return to_row(place, place, fwd_s.at[h, k], fwd_r.at[h, k], sibling)

    for h in range(PARTS):
        far_first(n_chip, lambda k: feat_copy(h, k, i).start())
        sib_copy(h, i).start()

    loads[0].wait()
    tiles[slots] = jnp.zeros((tile, tile), BF16)
    tiles_t[slots] = jnp.zeros((tile, tile), BF16)

    def flip(s):
        tiles_t[s] = tiles[s].T

    repeat(0, slots, flip)
    count = count_ref[0, 0]

    def place_row(r):
        def place(c):
            slot = jnp.int32(slots)
            for s in range(slots):
                hit = (rows_ref[0, 0, s] == r) & (cols_ref[0, 0, s] == c) & (s < count)
                slot = jnp.where(hit, jnp.int32(s), slot)
            adj[block(r, tile), block(c, tile)] = tiles[slot]
            adj_t[block(c, tile), block(r, tile)] = tiles_t[slot]

        repeat(0, col_tiles, place)

    repeat(0, row_tiles, place_row)
    for load in loads[1:]:
        load.wait()
    weight_t[...] = weight[...].T

    def part_copy(h, k):
        return to_col(part_send.at[h, k], part_recv.at[h, k],
                      part_s.at[h, k], part_r.at[h, k], col_peer(k))

    for h in range(PARTS):

        def pass_on(k):
            feat_copy(h, k, mate(k)).wait_recv()
            pass_copy(h, k, mate(k)).start()

        far_first(n_chip, pass_on)
        sib_copy(h, sibling).wait_recv()
        far_first(n_chip, lambda k: pass_copy(h, k, mate(k) + sibling - i).wait_recv())

        def forward(k):
            rows = block(col_peer(k), nodes)
            part_send[h, k] = dot(adj[rows, :], feat_all[h]).astype(BF16)
            part_copy(h, k).start()

        far_first(n_col, forward)
        part_recv[h, 0] = dot(adj[block(j, nodes), :], feat_all[h]).astype(BF16)

    gathered = []
    preact = jnp.zeros((nodes, width), F32)
    for h in range(PARTS):
        far_first(n_col, lambda k: part_copy(h, k).wait_recv())
        total = part_recv[h, 0].astype(F32)
        for k in range(1, n_col):
            total = total + part_recv[h, k].astype(F32)
        gathered.append(total.astype(BF16))
        preact = preact + dot(gathered[h], weight[strip(h), :])
    aggregate = jnp.concatenate(gathered, axis=1)
    value, slope = gelu_and_slope(preact)
    cotangent = (upstream[...].astype(F32) * slope).astype(BF16)

    def cot_copy(h, k, owner):
        place = cot_all.at[h, block(owner, nodes)]
        return to_col(place, place, cot_s.at[h, k], cot_r.at[h, k], col_peer(k))

    for h in range(PARTS):
        cot_all[h, block(j, nodes), :] = cotangent[:, h * lanes:(h + 1) * lanes]
        far_first(n_col, lambda k: cot_copy(h, k, j).start())
    act[...] = value.astype(BF16)
    act_store = pltpu.make_async_copy(act, act_out, out_sem.at[0])
    act_store.start()

    term = lax.dot_general(aggregate, cotangent, (((0,), (0,)), ((), ())),
                           preferred_element_type=F32)
    term = (term * (nodes * n_row * n_col) ** -0.5).astype(BF16)
    w_send[pl.ds(0, width), :] = term[:, :half]
    w_send[pl.ds(width, width), :] = term[:, half:]

    def w1_copy(k):
        return to_row(w_send.at[block(row_peer(k), piece)], w_recv.at[k],
                      w1_s.at[k], w1_r.at[k], row_peer(k))

    far_first(n_row, lambda k: w1_copy(k).start())
    w_recv[0] = w_send[block(i, piece), :]

    def pair_copy(h, k):
        return to_row(sib_send.at[h, k], sib_recv.at[h, k],
                      pair_s.at[h, k], pair_r.at[h, k], sibling)

    def back_copy(h, k):
        return to_row(back_send.at[h, k], back_recv.at[h, k],
                      back_s.at[h, k], back_r.at[h, k], mate(k))

    def back_dot(h, owner):
        return dot(adj_t[block(owner, nodes), :], cot_all[h])

    own = []
    for h in range(PARTS):
        far_first(n_col, lambda k: cot_copy(h, k, col_peer(k)).wait_recv())

        def to_sibling(k):
            sib_send[h, k] = back_dot(h, mate(k) + sibling - i).astype(BF16)
            pair_copy(h, k).start()

        def to_owner(k):
            mine = back_dot(h, mate(k))
            pair_copy(h, k).wait_recv()
            back_send[h, k] = (mine + sib_recv[h, k].astype(F32)).astype(BF16)
            back_copy(h, k).start()

        far_first(n_chip, to_sibling)
        to_sibling(0)
        far_first(n_chip, to_owner)
        mine = back_dot(h, i)
        pair_copy(h, 0).wait_recv()
        own.append(mine + sib_recv[h, 0].astype(F32))

    far_first(n_row, lambda k: w1_copy(k).wait_recv())
    summed = w_recv[0].astype(F32)
    for k in range(1, n_row):
        summed = summed + w_recv[k].astype(F32)
    w_mid[j] = summed.astype(BF16)

    def w2_copy(k, owner):
        return to_col(w_mid.at[owner], w_mid.at[owner], w2_s.at[k], w2_r.at[k], col_peer(k))

    far_first(n_col, lambda k: w2_copy(k, j).start())
    far_first(n_col, lambda k: w2_copy(k, col_peer(k)).wait_recv())
    summed = w_mid[0].astype(F32)
    for k in range(1, n_col):
        summed = summed + w_mid[k].astype(F32)
    w_all[block(i, piece), :] = summed.astype(BF16)

    def w3_copy(k, owner):
        place = w_all.at[block(owner, piece)]
        return to_row(place, place, w3_s.at[k], w3_r.at[k], row_peer(k))

    far_first(n_row, lambda k: w3_copy(k, i).start())

    grad = jnp.zeros((nodes, width), F32)
    for h in range(PARTS):
        far_first(n_chip, lambda k: back_copy(h, k).wait_recv())
        pulled = own[h]
        for k in range(1, n_chip):
            pulled = pulled + back_recv[h, k].astype(F32)
        grad = grad + dot(pulled.astype(BF16), weight_t[strip(h), :])
    fgrad[...] = grad.astype(BF16)
    fgrad_store = pltpu.make_async_copy(fgrad, fgrad_out, out_sem.at[1])
    fgrad_store.start()

    far_first(n_row, lambda k: w3_copy(k, row_peer(k)).wait_recv())
    wgrad[:, pl.ds(0, half)] = w_all[pl.ds(0, width), :].astype(F32)
    wgrad[:, pl.ds(half, half)] = w_all[pl.ds(width, width), :].astype(F32)
    wgrad_store = pltpu.make_async_copy(wgrad, wgrad_out, out_sem.at[2])
    wgrad_store.start()

    def row_sent(k):
        w1_copy(k).wait_send()
        w3_copy(k, i).wait_send()

    repeat(1, n_row, row_sent)
    repeat(1, n_col, lambda k: w2_copy(k, j).wait_send())
    for h in range(PARTS):

        def chip_sent(k):
            feat_copy(h, k, i).wait_send()
            pass_copy(h, k, mate(k)).wait_send()
            pair_copy(h, k).wait_send()
            back_copy(h, k).wait_send()

        def col_sent(k):
            part_copy(h, k).wait_send()
            cot_copy(h, k, j).wait_send()

        sib_copy(h, i).wait_send()
        pair_copy(h, 0).wait_send()
        repeat(1, n_chip, chip_sent)
        repeat(1, n_col, col_sent)
    act_store.wait()
    fgrad_store.wait()
    wgrad_store.wait()


def hand_over(*refs):
    sources, results, sems = refs[:3], refs[3:6], refs[6]
    copies = [
        pltpu.make_async_copy(source, result, sems.at[n])
        for n, (source, result) in enumerate(zip(sources, results))
    ]
    for copy in copies:
        copy.start()
    for copy in copies:
        copy.wait()


def body(features, tile_values, tile_rows, tile_cols, tile_count, weight, out_grad):
    n_row, n_col = lax.axis_size("row"), lax.axis_size("col")
    n_chip = n_row // 2
    nodes, width = features.shape
    slots, tile = tile_values.shape[2], tile_values.shape[3]
    tall, wide = n_col * nodes, n_row * nodes
    piece = 2 * width // n_row
    lanes = width // PARTS
    vmem, dma = pltpu.VMEM, pltpu.SemaphoreType.DMA
    anywhere = pl.BlockSpec(memory_space=pl.ANY)
    scalars = pl.BlockSpec(memory_space=pltpu.SMEM)
    shapes = (
        jax.ShapeDtypeStruct((nodes, width), BF16),
        jax.ShapeDtypeStruct((nodes, width), BF16),
        jax.ShapeDtypeStruct((width, width), F32),
    )
    results = pl.pallas_call(
        functools.partial(kernel, n_row, n_col),
        out_shape=shapes,
        in_specs=[anywhere, anywhere, scalars, scalars, scalars, anywhere, anywhere],
        out_specs=(anywhere, anywhere, anywhere),
        scratch_shapes=[
            vmem((PARTS, wide, lanes), BF16),
            vmem((slots + 1, tile, tile), BF16),
            vmem((slots + 1, tile, tile), BF16),
            vmem((tall, wide), BF16),
            vmem((wide, tall), BF16),
            vmem((width, width), BF16),
            vmem((width, width), BF16),
            vmem((nodes, width), BF16),
            vmem((PARTS, n_col, nodes, lanes), BF16),
            vmem((PARTS, n_col, nodes, lanes), BF16),
            vmem((PARTS, tall, lanes), BF16),
            vmem((PARTS, n_chip, nodes, lanes), BF16),
            vmem((PARTS, n_chip, nodes, lanes), BF16),
            vmem((PARTS, n_chip, nodes, lanes), BF16),
            vmem((PARTS, n_chip, nodes, lanes), BF16),
            vmem((2 * width, width // 2), BF16),
            vmem((n_row, piece, width // 2), BF16),
            vmem((n_col, piece, width // 2), BF16),
            vmem((2 * width, width // 2), BF16),
            vmem((nodes, width), BF16),
            vmem((nodes, width), BF16),
            vmem((width, width), F32),
            dma((3 + PARTS,)), dma((3,)), dma((PARTS,)), dma((PARTS,)),
        ]
        + [dma((PARTS, n_chip))] * 4
        + [dma((PARTS, n_col))] * 4
        + [dma((PARTS, n_chip))] * 4
        + [dma((n_row,))] * 2 + [dma((n_col,))] * 2 + [dma((n_row,))] * 2,
        compiler_params=pltpu.CompilerParams(
            collective_id=0, has_side_effects=True, vmem_limit_bytes=56 * 1024 * 1024),
    )(features, tile_values[0, 0], tile_rows, tile_cols, tile_count, weight, out_grad)
    return tuple(pl.pallas_call(
        hand_over,
        out_shape=shapes,
        in_specs=[anywhere] * 3,
        out_specs=(anywhere,) * 3,
        scratch_shapes=[dma((3,))],
    )(*results))


def solution(mesh):
    placed = (
        P(("row", "col"), None),
        P("row", "col", None, None, None),
        P("row", "col", None),
        P("row", "col", None),
        P("row", "col"),
        P(),
        P(("row", "col"), None),
    )
    return jax.shard_map(
        body,
        mesh=mesh,
        in_specs=placed,
        out_specs=(P(("row", "col"), None), P(("row", "col"), None), P()),
        check_vma=False,
    )
```

```python
import functools

import jax
import jax.numpy as jnp
from jax import lax
from jax.experimental import pallas as pl
from jax.experimental.pallas import tpu as pltpu
from jax.sharding import PartitionSpec as P

MESH = pl.DeviceIdType.MESH
F32 = jnp.float32
BF16 = jnp.bfloat16


def repeat(low, high, step):
    if high - low <= 8:
        for k in range(low, high):
            step(k)
    else:

        def once(k, carry):
            step(k)
            return carry

        lax.fori_loop(low, high, once, 0)


def block(index, size):
    if isinstance(index, int):
        return pl.ds(index * size, size)
    return pl.ds(pl.multiple_of(index * size, size), size)


def partner(rank, k, size):
    assert size & (size - 1) == 0
    found, bit = 0, 1
    while bit < size:
        found = found + bit * ((rank // bit + k // bit) % 2)
        bit *= 2
    return found


def far_first(size, step):
    repeat(1, size, lambda m: step(size - m))


def dot(a, b):
    return jnp.dot(a, b, preferred_element_type=F32)


def gelu_and_slope(v):
    scale = 0.7978845608028654
    square = v * v
    t = jnp.tanh(scale * (v + 0.044715 * v * square))
    half = 0.5 * (1.0 + t)
    slope = half + 0.5 * v * (1.0 - t * t) * scale * (1.0 + 3 * 0.044715 * square)
    return v * half, slope


PARTS = 1


def kernel(
    n_row, n_col,
    feat_in, tiles_in, rows_ref, cols_ref, count_ref, weight_in, upstream_in,
    act, fgrad, wgrad,
    feat_all, tiles, tiles_t, adj, adj_t, weight, weight_t, upstream,
    part_send, part_recv, cot_all, sib_send, sib_recv, back_send, back_recv,
    w_send, w_recv, w_mid, w_all,
    in_sem, sib_s, sib_r,
    feat_s, feat_r, fwd_s, fwd_r, part_s, part_r, cot_s, cot_r,
    pair_s, pair_r, back_s, back_r, w1_s, w1_r, w2_s, w2_r, w3_s, w3_r,
):
    i, j = lax.axis_index("row"), lax.axis_index("col")
    chip, core = i // 2, i % 2
    n_chip = n_row // 2
    sibling = 2 * chip + 1 - core
    nodes, width = feat_in.shape
    slots, tile = tiles_in.shape[0], tiles_in.shape[1]
    row_tiles = n_col * nodes // tile
    col_tiles = n_row * nodes // tile
    half = width // 2
    piece = 2 * width // n_row
    lanes = width // PARTS

    def to_row(src, dst, send, recv, peer):
        return pltpu.make_async_remote_copy(
            src_ref=src, dst_ref=dst, send_sem=send, recv_sem=recv,
            device_id=(peer, j), device_id_type=MESH)

    def to_col(src, dst, send, recv, peer):
        return pltpu.make_async_remote_copy(
            src_ref=src, dst_ref=dst, send_sem=send, recv_sem=recv,
            device_id=(i, peer), device_id_type=MESH)

    def row_peer(k):
        return partner(i, k, n_row)

    def col_peer(k):
        return partner(j, k, n_col)

    def mate(k):
        return 2 * partner(chip, k, n_chip) + core

    def strip(h):
        return pl.ds(h * lanes, lanes)

    loads = [
        pltpu.make_async_copy(tiles_in, tiles.at[pl.ds(0, slots)], in_sem.at[0]),
        pltpu.make_async_copy(weight_in, weight, in_sem.at[1]),
        pltpu.make_async_copy(upstream_in, upstream, in_sem.at[2]),
    ] + [
        pltpu.make_async_copy(feat_in.at[:, strip(h)], feat_all.at[h, block(i, nodes)],
                              in_sem.at[3 + h])
        for h in range(PARTS)
    ]
    for load in loads:
        load.start()

    barrier = pltpu.get_barrier_semaphore()
    repeat(1, n_row, lambda k: pl.semaphore_signal(
        barrier, inc=1, device_id=(row_peer(k), j), device_id_type=MESH))
    repeat(1, n_col, lambda k: pl.semaphore_signal(
        barrier, inc=1, device_id=(i, col_peer(k)), device_id_type=MESH))
    pl.semaphore_wait(barrier, n_row + n_col - 2)

    def feat_copy(h, k, owner):
        return to_row(feat_in.at[:, strip(h)], feat_all.at[h, block(owner, nodes)],
                      feat_s.at[h, k], feat_r.at[h, k], mate(k))

    def sib_copy(h, owner):
        return to_row(feat_in.at[:, strip(h)], feat_all.at[h, block(owner, nodes)],
                      sib_s.at[h], sib_r.at[h], sibling)

    def pass_copy(h, k, owner):
        place = feat_all.at[h, block(owner, nodes)]
        return to_row(place, place, fwd_s.at[h, k], fwd_r.at[h, k], sibling)

    for h in range(PARTS):
        far_first(n_chip, lambda k: feat_copy(h, k, i).start())
        sib_copy(h, i).start()

    loads[0].wait()
    tiles[slots] = jnp.zeros((tile, tile), BF16)
    tiles_t[slots] = jnp.zeros((tile, tile), BF16)

    def flip(s):
        tiles_t[s] = tiles[s].T

    repeat(0, slots, flip)
    count = count_ref[0, 0]

    def place_row(r):
        def place(c):
            slot = jnp.int32(slots)
            for s in range(slots):
                hit = (rows_ref[0, 0, s] == r) & (cols_ref[0, 0, s] == c) & (s < count)
                slot = jnp.where(hit, jnp.int32(s), slot)
            adj[block(r, tile), block(c, tile)] = tiles[slot]
            adj_t[block(c, tile), block(r, tile)] = tiles_t[slot]

        repeat(0, col_tiles, place)

    repeat(0, row_tiles, place_row)
    for load in loads[1:]:
        load.wait()
    weight_t[...] = weight[...].T

    def part_copy(h, k):
        return to_col(part_send.at[h, k], part_recv.at[h, k],
                      part_s.at[h, k], part_r.at[h, k], col_peer(k))

    for h in range(PARTS):

        def pass_on(k):
            feat_copy(h, k, mate(k)).wait_recv()
            pass_copy(h, k, mate(k)).start()

        far_first(n_chip, pass_on)
        sib_copy(h, sibling).wait_recv()
        far_first(n_chip, lambda k: pass_copy(h, k, mate(k) + sibling - i).wait_recv())

        def forward(k):
            rows = block(col_peer(k), nodes)
            part_send[h, k] = dot(adj[rows, :], feat_all[h]).astype(BF16)
            part_copy(h, k).start()

        far_first(n_col, forward)
        part_recv[h, 0] = dot(adj[block(j, nodes), :], feat_all[h]).astype(BF16)

    gathered = []
    preact = jnp.zeros((nodes, width), F32)
    for h in range(PARTS):
        far_first(n_col, lambda k: part_copy(h, k).wait_recv())
        total = part_recv[h, 0].astype(F32)
        for k in range(1, n_col):
            total = total + part_recv[h, k].astype(F32)
        gathered.append(total.astype(BF16))
        preact = preact + dot(gathered[h], weight[strip(h), :])
    aggregate = jnp.concatenate(gathered, axis=1)
    value, slope = gelu_and_slope(preact)
    cotangent = (upstream[...].astype(F32) * slope).astype(BF16)

    def cot_copy(h, k, owner):
        place = cot_all.at[h, block(owner, nodes)]
        return to_col(place, place, cot_s.at[h, k], cot_r.at[h, k], col_peer(k))

    for h in range(PARTS):
        cot_all[h, block(j, nodes), :] = cotangent[:, h * lanes:(h + 1) * lanes]
        far_first(n_col, lambda k: cot_copy(h, k, j).start())
    act[...] = value.astype(BF16)

    term = lax.dot_general(aggregate, cotangent, (((0,), (0,)), ((), ())),
                           preferred_element_type=F32)
    term = (term * (nodes * n_row * n_col) ** -0.5).astype(BF16)
    w_send[pl.ds(0, width), :] = term[:, :half]
    w_send[pl.ds(width, width), :] = term[:, half:]

    def w1_copy(k):
        return to_row(w_send.at[block(row_peer(k), piece)], w_recv.at[k],
                      w1_s.at[k], w1_r.at[k], row_peer(k))

    far_first(n_row, lambda k: w1_copy(k).start())
    w_recv[0] = w_send[block(i, piece), :]

    def pair_copy(h, k):
        return to_row(sib_send.at[h, k], sib_recv.at[h, k],
                      pair_s.at[h, k], pair_r.at[h, k], sibling)

    def back_copy(h, k):
        return to_row(back_send.at[h, k], back_recv.at[h, k],
                      back_s.at[h, k], back_r.at[h, k], mate(k))

    def back_dot(h, owner):
        return dot(adj_t[block(owner, nodes), :], cot_all[h])

    own = []
    for h in range(PARTS):
        far_first(n_col, lambda k: cot_copy(h, k, col_peer(k)).wait_recv())

        def to_sibling(k):
            sib_send[h, k] = back_dot(h, mate(k) + sibling - i).astype(BF16)
            pair_copy(h, k).start()

        def to_owner(k):
            mine = back_dot(h, mate(k))
            pair_copy(h, k).wait_recv()
            back_send[h, k] = (mine + sib_recv[h, k].astype(F32)).astype(BF16)
            back_copy(h, k).start()

        far_first(n_chip, to_sibling)
        to_sibling(0)
        far_first(n_chip, to_owner)
        mine = back_dot(h, i)
        pair_copy(h, 0).wait_recv()
        own.append(mine + sib_recv[h, 0].astype(F32))

    far_first(n_row, lambda k: w1_copy(k).wait_recv())
    summed = w_recv[0].astype(F32)
    for k in range(1, n_row):
        summed = summed + w_recv[k].astype(F32)
    w_mid[j] = summed.astype(BF16)

    def w2_copy(k, owner):
        return to_col(w_mid.at[owner], w_mid.at[owner], w2_s.at[k], w2_r.at[k], col_peer(k))

    far_first(n_col, lambda k: w2_copy(k, j).start())
    far_first(n_col, lambda k: w2_copy(k, col_peer(k)).wait_recv())
    summed = w_mid[0].astype(F32)
    for k in range(1, n_col):
        summed = summed + w_mid[k].astype(F32)
    w_all[block(i, piece), :] = summed.astype(BF16)

    def w3_copy(k, owner):
        place = w_all.at[block(owner, piece)]
        return to_row(place, place, w3_s.at[k], w3_r.at[k], row_peer(k))

    far_first(n_row, lambda k: w3_copy(k, i).start())

    grad = jnp.zeros((nodes, width), F32)
    for h in range(PARTS):
        far_first(n_chip, lambda k: back_copy(h, k).wait_recv())
        pulled = own[h]
        for k in range(1, n_chip):
            pulled = pulled + back_recv[h, k].astype(F32)
        grad = grad + dot(pulled.astype(BF16), weight_t[strip(h), :])
    fgrad[...] = grad.astype(BF16)

    far_first(n_row, lambda k: w3_copy(k, row_peer(k)).wait_recv())
    wgrad[:, pl.ds(0, half)] = w_all[pl.ds(0, width), :].astype(F32)
    wgrad[:, pl.ds(half, half)] = w_all[pl.ds(width, width), :].astype(F32)

    def row_sent(k):
        w1_copy(k).wait_send()
        w3_copy(k, i).wait_send()

    repeat(1, n_row, row_sent)
    repeat(1, n_col, lambda k: w2_copy(k, j).wait_send())
    for h in range(PARTS):

        def chip_sent(k):
            feat_copy(h, k, i).wait_send()
            pass_copy(h, k, mate(k)).wait_send()
            pair_copy(h, k).wait_send()
            back_copy(h, k).wait_send()

        def col_sent(k):
            part_copy(h, k).wait_send()
            cot_copy(h, k, j).wait_send()

        sib_copy(h, i).wait_send()
        pair_copy(h, 0).wait_send()
        repeat(1, n_chip, chip_sent)
        repeat(1, n_col, col_sent)


def hand_over(*refs):
    sources, results, sems = refs[:3], refs[3:6], refs[6]
    copies = [
        pltpu.make_async_copy(source, result, sems.at[n])
        for n, (source, result) in enumerate(zip(sources, results))
    ]
    for copy in copies:
        copy.start()
    for copy in copies:
        copy.wait()


def body(features, tile_values, tile_rows, tile_cols, tile_count, weight, out_grad):
    n_row, n_col = lax.axis_size("row"), lax.axis_size("col")
    n_chip = n_row // 2
    nodes, width = features.shape
    slots, tile = tile_values.shape[2], tile_values.shape[3]
    tall, wide = n_col * nodes, n_row * nodes
    piece = 2 * width // n_row
    lanes = width // PARTS
    vmem, dma = pltpu.VMEM, pltpu.SemaphoreType.DMA
    anywhere = pl.BlockSpec(memory_space=pl.ANY)
    in_vmem = pl.BlockSpec(memory_space=pltpu.VMEM)
    scalars = pl.BlockSpec(memory_space=pltpu.SMEM)
    shapes = (
        jax.ShapeDtypeStruct((nodes, width), BF16),
        jax.ShapeDtypeStruct((nodes, width), BF16),
        jax.ShapeDtypeStruct((width, width), F32),
    )
    results = pl.pallas_call(
        functools.partial(kernel, n_row, n_col),
        out_shape=tuple(pltpu.VMEM(s.shape, s.dtype) for s in shapes),
        in_specs=[anywhere, anywhere, scalars, scalars, scalars, anywhere, anywhere],
        out_specs=(in_vmem,) * 3,
        scratch_shapes=[
            vmem((PARTS, wide, lanes), BF16),
            vmem((slots + 1, tile, tile), BF16),
            vmem((slots + 1, tile, tile), BF16),
            vmem((tall, wide), BF16),
            vmem((wide, tall), BF16),
            vmem((width, width), BF16),
            vmem((width, width), BF16),
            vmem((nodes, width), BF16),
            vmem((PARTS, n_col, nodes, lanes), BF16),
            vmem((PARTS, n_col, nodes, lanes), BF16),
            vmem((PARTS, tall, lanes), BF16),
            vmem((PARTS, n_chip, nodes, lanes), BF16),
            vmem((PARTS, n_chip, nodes, lanes), BF16),
            vmem((PARTS, n_chip, nodes, lanes), BF16),
            vmem((PARTS, n_chip, nodes, lanes), BF16),
            vmem((2 * width, width // 2), BF16),
            vmem((n_row, piece, width // 2), BF16),
            vmem((n_col, piece, width // 2), BF16),
            vmem((2 * width, width // 2), BF16),
            dma((3 + PARTS,)), dma((PARTS,)), dma((PARTS,)),
        ]
        + [dma((PARTS, n_chip))] * 4
        + [dma((PARTS, n_col))] * 4
        + [dma((PARTS, n_chip))] * 4
        + [dma((n_row,))] * 2 + [dma((n_col,))] * 2 + [dma((n_row,))] * 2,
        compiler_params=pltpu.CompilerParams(
            collective_id=0, has_side_effects=True, vmem_limit_bytes=56 * 1024 * 1024),
    )(features, tile_values[0, 0], tile_rows, tile_cols, tile_count, weight, out_grad)
    return tuple(pl.pallas_call(
        hand_over,
        out_shape=shapes,
        in_specs=[in_vmem] * 3,
        out_specs=(anywhere,) * 3,
        scratch_shapes=[dma((3,))],
    )(*results))


def solution(mesh):
    placed = (
        P(("row", "col"), None),
        P("row", "col", None, None, None),
        P("row", "col", None),
        P("row", "col", None),
        P("row", "col"),
        P(),
        P(("row", "col"), None),
    )
    return jax.shard_map(
        body,
        mesh=mesh,
        in_specs=placed,
        out_specs=(P(("row", "col"), None), P(("row", "col"), None), P()),
        check_vma=False,
    )
```

```python
import functools

import jax
import jax.numpy as jnp
from jax import lax
from jax.experimental import pallas as pl
from jax.experimental.pallas import tpu as pltpu
from jax.sharding import PartitionSpec as P

MESH = pl.DeviceIdType.MESH
F32 = jnp.float32
BF16 = jnp.bfloat16


def repeat(low, high, step):
    if high - low <= 8:
        for k in range(low, high):
            step(k)
    else:

        def once(k, carry):
            step(k)
            return carry

        lax.fori_loop(low, high, once, 0)


def block(index, size):
    if isinstance(index, int):
        return pl.ds(index * size, size)
    return pl.ds(pl.multiple_of(index * size, size), size)


def partner(rank, k, size):
    assert size & (size - 1) == 0
    found, bit = 0, 1
    while bit < size:
        found = found + bit * ((rank // bit + k // bit) % 2)
        bit *= 2
    return found


def far_first(size, step):
    repeat(1, size, lambda m: step(size - m))


def dot(a, b):
    return jnp.dot(a, b, preferred_element_type=F32)


def gelu_and_slope(v):
    scale = 0.7978845608028654
    square = v * v
    t = jnp.tanh(scale * (v + 0.044715 * v * square))
    half = 0.5 * (1.0 + t)
    slope = half + 0.5 * v * (1.0 - t * t) * scale * (1.0 + 3 * 0.044715 * square)
    return v * half, slope


PARTS = 2


def kernel(
    n_row, n_col,
    feat_in, tiles_in, rows_ref, cols_ref, count_ref, weight_in, upstream_in,
    act, fgrad, wgrad,
    feat_all, tiles, tiles_t, adj, adj_t, weight, weight_t, upstream,
    part_send, part_recv, cot_all, sib_send, sib_recv, back_send, back_recv,
    w_send, w_recv, w_mid, w_all,
    in_sem, sib_s, sib_r,
    feat_s, feat_r, fwd_s, fwd_r, part_s, part_r, cot_s, cot_r,
    pair_s, pair_r, back_s, back_r, w1_s, w1_r, w2_s, w2_r, w3_s, w3_r,
):
    i, j = lax.axis_index("row"), lax.axis_index("col")
    chip, core = i // 2, i % 2
    n_chip = n_row // 2
    sibling = 2 * chip + 1 - core
    nodes, width = feat_in.shape
    slots, tile = tiles_in.shape[0], tiles_in.shape[1]
    row_tiles = n_col * nodes // tile
    col_tiles = n_row * nodes // tile
    half = width // 2
    piece = 2 * width // n_row
    lanes = width // PARTS

    def to_row(src, dst, send, recv, peer):
        return pltpu.make_async_remote_copy(
            src_ref=src, dst_ref=dst, send_sem=send, recv_sem=recv,
            device_id=(peer, j), device_id_type=MESH)

    def to_col(src, dst, send, recv, peer):
        return pltpu.make_async_remote_copy(
            src_ref=src, dst_ref=dst, send_sem=send, recv_sem=recv,
            device_id=(i, peer), device_id_type=MESH)

    def row_peer(k):
        return partner(i, k, n_row)

    def col_peer(k):
        return partner(j, k, n_col)

    def mate(k):
        return 2 * partner(chip, k, n_chip) + core

    def strip(h):
        return pl.ds(h * lanes, lanes)

    loads = [
        pltpu.make_async_copy(tiles_in, tiles.at[pl.ds(0, slots)], in_sem.at[0]),
        pltpu.make_async_copy(weight_in, weight, in_sem.at[1]),
        pltpu.make_async_copy(upstream_in, upstream, in_sem.at[2]),
    ] + [
        pltpu.make_async_copy(feat_in.at[:, strip(h)], feat_all.at[h, block(i, nodes)],
                              in_sem.at[3 + h])
        for h in range(PARTS)
    ]
    for load in loads:
        load.start()

    barrier = pltpu.get_barrier_semaphore()
    repeat(1, n_row, lambda k: pl.semaphore_signal(
        barrier, inc=1, device_id=(row_peer(k), j), device_id_type=MESH))
    repeat(1, n_col, lambda k: pl.semaphore_signal(
        barrier, inc=1, device_id=(i, col_peer(k)), device_id_type=MESH))
    pl.semaphore_wait(barrier, n_row + n_col - 2)

    def feat_copy(h, k, owner):
        return to_row(feat_in.at[:, strip(h)], feat_all.at[h, block(owner, nodes)],
                      feat_s.at[h, k], feat_r.at[h, k], mate(k))

    def sib_copy(h, owner):
        return to_row(feat_in.at[:, strip(h)], feat_all.at[h, block(owner, nodes)],
                      sib_s.at[h], sib_r.at[h], sibling)

    def pass_copy(h, k, owner):
        place = feat_all.at[h, block(owner, nodes)]
        return to_row(place, place, fwd_s.at[h, k], fwd_r.at[h, k], sibling)

    for h in range(PARTS):
        far_first(n_chip, lambda k: feat_copy(h, k, i).start())
        sib_copy(h, i).start()

    loads[0].wait()
    tiles[slots] = jnp.zeros((tile, tile), BF16)
    tiles_t[slots] = jnp.zeros((tile, tile), BF16)

    def flip(s):
        tiles_t[s] = tiles[s].T

    repeat(0, slots, flip)
    count = count_ref[0, 0]

    def place_row(r):
        def place(c):
            slot = jnp.int32(slots)
            for s in range(slots):
                hit = (rows_ref[0, 0, s] == r) & (cols_ref[0, 0, s] == c) & (s < count)
                slot = jnp.where(hit, jnp.int32(s), slot)
            adj[block(r, tile), block(c, tile)] = tiles[slot]
            adj_t[block(c, tile), block(r, tile)] = tiles_t[slot]

        repeat(0, col_tiles, place)

    repeat(0, row_tiles, place_row)
    for load in loads[1:]:
        load.wait()
    weight_t[...] = weight[...].T

    def part_copy(h, k):
        return to_col(part_send.at[h, k], part_recv.at[h, k],
                      part_s.at[h, k], part_r.at[h, k], col_peer(k))

    for h in range(PARTS):

        def pass_on(k):
            feat_copy(h, k, mate(k)).wait_recv()
            pass_copy(h, k, mate(k)).start()

        far_first(n_chip, pass_on)
        sib_copy(h, sibling).wait_recv()
        far_first(n_chip, lambda k: pass_copy(h, k, mate(k) + sibling - i).wait_recv())

        def forward(k):
            rows = block(col_peer(k), nodes)
            part_send[h, k] = dot(adj[rows, :], feat_all[h]).astype(BF16)
            part_copy(h, k).start()

        far_first(n_col, forward)
        part_recv[h, 0] = dot(adj[block(j, nodes), :], feat_all[h]).astype(BF16)

    gathered = []
    preact = jnp.zeros((nodes, width), F32)
    for h in range(PARTS):
        far_first(n_col, lambda k: part_copy(h, k).wait_recv())
        total = part_recv[h, 0].astype(F32)
        for k in range(1, n_col):
            total = total + part_recv[h, k].astype(F32)
        gathered.append(total.astype(BF16))
        preact = preact + dot(gathered[h], weight[strip(h), :])
    aggregate = jnp.concatenate(gathered, axis=1)
    value, slope = gelu_and_slope(preact)
    cotangent = (upstream[...].astype(F32) * slope).astype(BF16)

    def cot_copy(h, k, owner):
        place = cot_all.at[h, block(owner, nodes)]
        return to_col(place, place, cot_s.at[h, k], cot_r.at[h, k], col_peer(k))

    for h in range(PARTS):
        cot_all[h, block(j, nodes), :] = cotangent[:, h * lanes:(h + 1) * lanes]
        far_first(n_col, lambda k: cot_copy(h, k, j).start())
    act[...] = value.astype(BF16)

    term = lax.dot_general(aggregate, cotangent, (((0,), (0,)), ((), ())),
                           preferred_element_type=F32)
    term = (term * (nodes * n_row * n_col) ** -0.5).astype(BF16)
    w_send[pl.ds(0, width), :] = term[:, :half]
    w_send[pl.ds(width, width), :] = term[:, half:]

    def w1_copy(k):
        return to_row(w_send.at[block(row_peer(k), piece)], w_recv.at[k],
                      w1_s.at[k], w1_r.at[k], row_peer(k))

    far_first(n_row, lambda k: w1_copy(k).start())
    w_recv[0] = w_send[block(i, piece), :]

    def pair_copy(h, k):
        return to_row(sib_send.at[h, k], sib_recv.at[h, k],
                      pair_s.at[h, k], pair_r.at[h, k], sibling)

    def back_copy(h, k):
        return to_row(back_send.at[h, k], back_recv.at[h, k],
                      back_s.at[h, k], back_r.at[h, k], mate(k))

    def back_dot(h, owner):
        return dot(adj_t[block(owner, nodes), :], cot_all[h])

    own = []
    for h in range(PARTS):
        far_first(n_col, lambda k: cot_copy(h, k, col_peer(k)).wait_recv())

        def to_sibling(k):
            sib_send[h, k] = back_dot(h, mate(k) + sibling - i).astype(BF16)
            pair_copy(h, k).start()

        def to_owner(k):
            mine = back_dot(h, mate(k))
            pair_copy(h, k).wait_recv()
            back_send[h, k] = (mine + sib_recv[h, k].astype(F32)).astype(BF16)
            back_copy(h, k).start()

        far_first(n_chip, to_sibling)
        to_sibling(0)
        far_first(n_chip, to_owner)
        mine = back_dot(h, i)
        pair_copy(h, 0).wait_recv()
        own.append(mine + sib_recv[h, 0].astype(F32))

    far_first(n_row, lambda k: w1_copy(k).wait_recv())
    summed = w_recv[0].astype(F32)
    for k in range(1, n_row):
        summed = summed + w_recv[k].astype(F32)
    w_mid[j] = summed.astype(BF16)

    def w2_copy(k, owner):
        return to_col(w_mid.at[owner], w_mid.at[owner], w2_s.at[k], w2_r.at[k], col_peer(k))

    far_first(n_col, lambda k: w2_copy(k, j).start())
    far_first(n_col, lambda k: w2_copy(k, col_peer(k)).wait_recv())
    summed = w_mid[0].astype(F32)
    for k in range(1, n_col):
        summed = summed + w_mid[k].astype(F32)
    w_all[block(i, piece), :] = summed.astype(BF16)

    def w3_copy(k, owner):
        place = w_all.at[block(owner, piece)]
        return to_row(place, place, w3_s.at[k], w3_r.at[k], row_peer(k))

    far_first(n_row, lambda k: w3_copy(k, i).start())

    grad = jnp.zeros((nodes, width), F32)
    for h in range(PARTS):
        far_first(n_chip, lambda k: back_copy(h, k).wait_recv())
        pulled = own[h]
        for k in range(1, n_chip):
            pulled = pulled + back_recv[h, k].astype(F32)
        grad = grad + dot(pulled.astype(BF16), weight_t[strip(h), :])
    fgrad[...] = grad.astype(BF16)

    far_first(n_row, lambda k: w3_copy(k, row_peer(k)).wait_recv())
    wgrad[:, pl.ds(0, half)] = w_all[pl.ds(0, width), :].astype(F32)
    wgrad[:, pl.ds(half, half)] = w_all[pl.ds(width, width), :].astype(F32)

    def row_sent(k):
        w1_copy(k).wait_send()
        w3_copy(k, i).wait_send()

    repeat(1, n_row, row_sent)
    repeat(1, n_col, lambda k: w2_copy(k, j).wait_send())
    for h in range(PARTS):

        def chip_sent(k):
            feat_copy(h, k, i).wait_send()
            pass_copy(h, k, mate(k)).wait_send()
            pair_copy(h, k).wait_send()
            back_copy(h, k).wait_send()

        def col_sent(k):
            part_copy(h, k).wait_send()
            cot_copy(h, k, j).wait_send()

        sib_copy(h, i).wait_send()
        pair_copy(h, 0).wait_send()
        repeat(1, n_chip, chip_sent)
        repeat(1, n_col, col_sent)


def hand_over(*refs):
    sources, results, sems = refs[:3], refs[3:6], refs[6]
    copies = [
        pltpu.make_async_copy(source, result, sems.at[n])
        for n, (source, result) in enumerate(zip(sources, results))
    ]
    for copy in copies:
        copy.start()
    for copy in copies:
        copy.wait()


def body(features, tile_values, tile_rows, tile_cols, tile_count, weight, out_grad):
    n_row, n_col = lax.axis_size("row"), lax.axis_size("col")
    n_chip = n_row // 2
    nodes, width = features.shape
    slots, tile = tile_values.shape[2], tile_values.shape[3]
    tall, wide = n_col * nodes, n_row * nodes
    piece = 2 * width // n_row
    lanes = width // PARTS
    vmem, dma = pltpu.VMEM, pltpu.SemaphoreType.DMA
    anywhere = pl.BlockSpec(memory_space=pl.ANY)
    in_vmem = pl.BlockSpec(memory_space=pltpu.VMEM)
    scalars = pl.BlockSpec(memory_space=pltpu.SMEM)
    shapes = (
        jax.ShapeDtypeStruct((nodes, width), BF16),
        jax.ShapeDtypeStruct((nodes, width), BF16),
        jax.ShapeDtypeStruct((width, width), F32),
    )
    results = pl.pallas_call(
        functools.partial(kernel, n_row, n_col),
        out_shape=tuple(pltpu.VMEM(s.shape, s.dtype) for s in shapes),
        in_specs=[anywhere, anywhere, scalars, scalars, scalars, anywhere, anywhere],
        out_specs=(in_vmem,) * 3,
        scratch_shapes=[
            vmem((PARTS, wide, lanes), BF16),
            vmem((slots + 1, tile, tile), BF16),
            vmem((slots + 1, tile, tile), BF16),
            vmem((tall, wide), BF16),
            vmem((wide, tall), BF16),
            vmem((width, width), BF16),
            vmem((width, width), BF16),
            vmem((nodes, width), BF16),
            vmem((PARTS, n_col, nodes, lanes), BF16),
            vmem((PARTS, n_col, nodes, lanes), BF16),
            vmem((PARTS, tall, lanes), BF16),
            vmem((PARTS, n_chip, nodes, lanes), BF16),
            vmem((PARTS, n_chip, nodes, lanes), BF16),
            vmem((PARTS, n_chip, nodes, lanes), BF16),
            vmem((PARTS, n_chip, nodes, lanes), BF16),
            vmem((2 * width, width // 2), BF16),
            vmem((n_row, piece, width // 2), BF16),
            vmem((n_col, piece, width // 2), BF16),
            vmem((2 * width, width // 2), BF16),
            dma((3 + PARTS,)), dma((PARTS,)), dma((PARTS,)),
        ]
        + [dma((PARTS, n_chip))] * 4
        + [dma((PARTS, n_col))] * 4
        + [dma((PARTS, n_chip))] * 4
        + [dma((n_row,))] * 2 + [dma((n_col,))] * 2 + [dma((n_row,))] * 2,
        compiler_params=pltpu.CompilerParams(
            collective_id=0, has_side_effects=True, vmem_limit_bytes=56 * 1024 * 1024),
    )(features, tile_values[0, 0], tile_rows, tile_cols, tile_count, weight, out_grad)
    return tuple(pl.pallas_call(
        hand_over,
        out_shape=shapes,
        in_specs=[in_vmem] * 3,
        out_specs=(anywhere,) * 3,
        scratch_shapes=[dma((3,))],
    )(*results))


def solution(mesh):
    placed = (
        P(("row", "col"), None),
        P("row", "col", None, None, None),
        P("row", "col", None),
        P("row", "col", None),
        P("row", "col"),
        P(),
        P(("row", "col"), None),
    )
    return jax.shard_map(
        body,
        mesh=mesh,
        in_specs=placed,
        out_specs=(P(("row", "col"), None), P(("row", "col"), None), P()),
        check_vma=False,
    )
```

```python
import functools

import jax
import jax.numpy as jnp
from jax import lax
from jax.experimental import pallas as pl
from jax.experimental.pallas import tpu as pltpu
from jax.sharding import PartitionSpec as P

MESH = pl.DeviceIdType.MESH
F32 = jnp.float32
BF16 = jnp.bfloat16


def repeat(low, high, step):
    if high - low <= 8:
        for k in range(low, high):
            step(k)
    else:

        def once(k, carry):
            step(k)
            return carry

        lax.fori_loop(low, high, once, 0)


def block(index, size):
    if isinstance(index, int):
        return pl.ds(index * size, size)
    return pl.ds(pl.multiple_of(index * size, size), size)


def partner(rank, k, size):
    assert size & (size - 1) == 0
    found, bit = 0, 1
    while bit < size:
        found = found + bit * ((rank // bit + k // bit) % 2)
        bit *= 2
    return found


def far_first(size, step):
    repeat(1, size, lambda m: step(size - m))


def dot(a, b):
    return jnp.dot(a, b, preferred_element_type=F32)


def gelu_and_slope(v):
    scale = 0.7978845608028654
    square = v * v
    t = jnp.tanh(scale * (v + 0.044715 * v * square))
    half = 0.5 * (1.0 + t)
    slope = half + 0.5 * v * (1.0 - t * t) * scale * (1.0 + 3 * 0.044715 * square)
    return v * half, slope


PARTS = 2


def kernel(
    n_row, n_col,
    feat_in, tiles_in, rows_ref, cols_ref, count_ref, weight_in, upstream_in,
    act, fgrad, wgrad,
    feat_all, tiles, tiles_t, adj, adj_t, weight, weight_t, upstream,
    part_send, part_recv, cot_all, sib_send, sib_recv, back_send, back_recv,
    w_send, w_recv, w_mid, w_all, slot_of,
    in_sem, sib_s, sib_r,
    feat_s, feat_r, fwd_s, fwd_r, part_s, part_r, cot_s, cot_r,
    pair_s, pair_r, back_s, back_r, w1_s, w1_r, w2_s, w2_r, w3_s, w3_r,
):
    i, j = lax.axis_index("row"), lax.axis_index("col")
    chip, core = i // 2, i % 2
    n_chip = n_row // 2
    sibling = 2 * chip + 1 - core
    nodes, width = feat_in.shape
    slots, tile = tiles_in.shape[0], tiles_in.shape[1]
    row_tiles = n_col * nodes // tile
    col_tiles = n_row * nodes // tile
    half = width // 2
    piece = 2 * width // n_row
    lanes = width // PARTS

    def to_row(src, dst, send, recv, peer):
        return pltpu.make_async_remote_copy(
            src_ref=src, dst_ref=dst, send_sem=send, recv_sem=recv,
            device_id=(peer, j), device_id_type=MESH)

    def to_col(src, dst, send, recv, peer):
        return pltpu.make_async_remote_copy(
            src_ref=src, dst_ref=dst, send_sem=send, recv_sem=recv,
            device_id=(i, peer), device_id_type=MESH)

    def row_peer(k):
        return partner(i, k, n_row)

    def col_peer(k):
        return partner(j, k, n_col)

    def mate(k):
        return 2 * partner(chip, k, n_chip) + core

    def strip(h):
        return pl.ds(h * lanes, lanes)

    loads = [
        pltpu.make_async_copy(tiles_in, tiles.at[pl.ds(0, slots)], in_sem.at[0]),
        pltpu.make_async_copy(weight_in, weight, in_sem.at[1]),
        pltpu.make_async_copy(upstream_in, upstream, in_sem.at[2]),
    ] + [
        pltpu.make_async_copy(feat_in.at[:, strip(h)], feat_all.at[h, block(i, nodes)],
                              in_sem.at[3 + h])
        for h in range(PARTS)
    ]
    for load in loads:
        load.start()

    barrier = pltpu.get_barrier_semaphore()
    repeat(1, n_row, lambda k: pl.semaphore_signal(
        barrier, inc=1, device_id=(row_peer(k), j), device_id_type=MESH))
    repeat(1, n_col, lambda k: pl.semaphore_signal(
        barrier, inc=1, device_id=(i, col_peer(k)), device_id_type=MESH))
    count = count_ref[0, 0]

    def find_row(r):
        def find(c):
            slot = jnp.int32(slots)
            for s in range(slots):
                hit = (rows_ref[0, 0, s] == r) & (cols_ref[0, 0, s] == c) & (s < count)
                slot = jnp.where(hit, jnp.int32(s), slot)
            slot_of[r * col_tiles + c] = slot

        repeat(0, col_tiles, find)

    repeat(0, row_tiles, find_row)
    tiles[slots] = jnp.zeros((tile, tile), BF16)
    tiles_t[slots] = jnp.zeros((tile, tile), BF16)
    pl.semaphore_wait(barrier, n_row + n_col - 2)

    def feat_copy(h, k, owner):
        return to_row(feat_in.at[:, strip(h)], feat_all.at[h, block(owner, nodes)],
                      feat_s.at[h, k], feat_r.at[h, k], mate(k))

    def sib_copy(h, owner):
        return to_row(feat_in.at[:, strip(h)], feat_all.at[h, block(owner, nodes)],
                      sib_s.at[h], sib_r.at[h], sibling)

    def pass_copy(h, k, owner):
        place = feat_all.at[h, block(owner, nodes)]
        return to_row(place, place, fwd_s.at[h, k], fwd_r.at[h, k], sibling)

    for h in range(PARTS):
        far_first(n_chip, lambda k: feat_copy(h, k, i).start())
        sib_copy(h, i).start()

    loads[0].wait()

    def place_row(r):
        def place(c):
            adj[block(r, tile), block(c, tile)] = tiles[slot_of[r * col_tiles + c]]

        repeat(0, col_tiles, place)

    repeat(0, row_tiles, place_row)
    for load in loads[3:]:
        load.wait()

    def part_copy(h, k):
        return to_col(part_send.at[h, block(col_peer(k), nodes)], part_recv.at[h, k],
                      part_s.at[h, k], part_r.at[h, k], col_peer(k))

    for h in range(PARTS):

        def pass_on(k):
            feat_copy(h, k, mate(k)).wait_recv()
            pass_copy(h, k, mate(k)).start()

        far_first(n_chip, pass_on)
        sib_copy(h, sibling).wait_recv()
        far_first(n_chip, lambda k: pass_copy(h, k, mate(k) + sibling - i).wait_recv())

        part_send[h] = dot(adj[...], feat_all[h]).astype(BF16)
        far_first(n_col, lambda k: part_copy(h, k).start())
        part_recv[h, 0] = part_send[h, block(j, nodes), :]

    def flip(s):
        tiles_t[s] = tiles[s].T

    repeat(0, slots, flip)
    per = nodes // tile

    def place_back(r):
        def place(c):
            rank = c // per
            spot = ((rank % 2) * n_chip + rank // 2) * per + c % per
            adj_t[block(spot, tile), block(r, tile)] = tiles_t[slot_of[r * col_tiles + c]]

        repeat(0, col_tiles, place)

    repeat(0, row_tiles, place_back)
    loads[1].wait()
    loads[2].wait()
    weight_t[...] = weight[...].T
    for h in range(PARTS):

        def feat_sent(k):
            feat_copy(h, k, i).wait_send()
            pass_copy(h, k, mate(k)).wait_send()

        sib_copy(h, i).wait_send()
        repeat(1, n_chip, feat_sent)

    gathered = []
    preact = jnp.zeros((nodes, width), F32)
    for h in range(PARTS):
        far_first(n_col, lambda k: part_copy(h, k).wait_recv())
        total = part_recv[h, 0].astype(F32)
        for k in range(1, n_col):
            total = total + part_recv[h, k].astype(F32)
        gathered.append(total.astype(BF16))
        preact = preact + dot(gathered[h], weight[strip(h), :])
    aggregate = jnp.concatenate(gathered, axis=1)
    value, slope = gelu_and_slope(preact)
    cotangent = (upstream[...].astype(F32) * slope).astype(BF16)

    def cot_copy(h, k, owner):
        place = cot_all.at[h, block(owner, nodes)]
        return to_col(place, place, cot_s.at[h, k], cot_r.at[h, k], col_peer(k))

    for h in range(PARTS):
        cot_all[h, block(j, nodes), :] = cotangent[:, h * lanes:(h + 1) * lanes]
        far_first(n_col, lambda k: cot_copy(h, k, j).start())
    act[...] = value.astype(BF16)

    term = lax.dot_general(aggregate, cotangent, (((0,), (0,)), ((), ())),
                           preferred_element_type=F32)
    term = (term * (nodes * n_row * n_col) ** -0.5).astype(BF16)
    w_send[pl.ds(0, width), :] = term[:, :half]
    w_send[pl.ds(width, width), :] = term[:, half:]

    def w1_copy(k):
        return to_row(w_send.at[block(row_peer(k), piece)], w_recv.at[k],
                      w1_s.at[k], w1_r.at[k], row_peer(k))

    far_first(n_row, lambda k: w1_copy(k).start())
    w_recv[0] = w_send[block(i, piece), :]
    for h in range(PARTS):
        repeat(1, n_col, lambda k: part_copy(h, k).wait_send())

    def w2_copy(k, owner):
        return to_col(w_mid.at[owner], w_mid.at[owner], w2_s.at[k], w2_r.at[k], col_peer(k))

    def w3_copy(k, owner):
        place = w_all.at[block(owner, piece)]
        return to_row(place, place, w3_s.at[k], w3_r.at[k], row_peer(k))

    def sum_over_row():
        far_first(n_row, lambda k: w1_copy(k).wait_recv())
        summed = w_recv[0].astype(F32)
        for k in range(1, n_row):
            summed = summed + w_recv[k].astype(F32)
        w_mid[j] = summed.astype(BF16)
        far_first(n_col, lambda k: w2_copy(k, j).start())

    def sum_over_col():
        far_first(n_col, lambda k: w2_copy(k, col_peer(k)).wait_recv())
        summed = w_mid[0].astype(F32)
        for k in range(1, n_col):
            summed = summed + w_mid[k].astype(F32)
        w_all[block(i, piece), :] = summed.astype(BF16)
        far_first(n_row, lambda k: w3_copy(k, i).start())

    def pair_copy(h):
        return to_row(sib_send.at[h], sib_recv.at[h], pair_s.at[h], pair_r.at[h], sibling)

    def back_copy(h, k):
        return to_row(back_send.at[h, block(partner(chip, k, n_chip), nodes)],
                      back_recv.at[h, k], back_s.at[h, k], back_r.at[h, k], mate(k))

    for h in range(PARTS):
        far_first(n_col, lambda k: cot_copy(h, k, col_peer(k)).wait_recv())
        sib_send[h] = dot(adj_t[block(1 - core, n_chip * nodes), :], cot_all[h]).astype(BF16)
        pair_copy(h).start()
        mine = dot(adj_t[block(core, n_chip * nodes), :], cot_all[h])
        pair_copy(h).wait_recv()
        back_send[h] = (mine + sib_recv[h].astype(F32)).astype(BF16)
        far_first(n_chip, lambda k: back_copy(h, k).start())
        if h == 0:
            sum_over_row()
    sum_over_col()
    for h in range(PARTS):
        pair_copy(h).wait_send()
        repeat(1, n_col, lambda k: cot_copy(h, k, j).wait_send())
    repeat(1, n_row, lambda k: w1_copy(k).wait_send())
    repeat(1, n_col, lambda k: w2_copy(k, j).wait_send())

    grad = jnp.zeros((nodes, width), F32)
    for h in range(PARTS):
        far_first(n_chip, lambda k: back_copy(h, k).wait_recv())
        pulled = back_send[h, block(chip, nodes), :].astype(F32)
        for k in range(1, n_chip):
            pulled = pulled + back_recv[h, k].astype(F32)
        grad = grad + dot(pulled.astype(BF16), weight_t[strip(h), :])
    fgrad[...] = grad.astype(BF16)

    far_first(n_row, lambda k: w3_copy(k, row_peer(k)).wait_recv())
    wgrad[:, pl.ds(0, half)] = w_all[pl.ds(0, width), :].astype(F32)
    wgrad[:, pl.ds(half, half)] = w_all[pl.ds(width, width), :].astype(F32)

    repeat(1, n_row, lambda k: w3_copy(k, i).wait_send())
    for h in range(PARTS):
        repeat(1, n_chip, lambda k: back_copy(h, k).wait_send())


def hand_over(*refs):
    sources, results, sems = refs[:3], refs[3:6], refs[6]
    copies = [
        pltpu.make_async_copy(source, result, sems.at[n])
        for n, (source, result) in enumerate(zip(sources, results))
    ]
    for copy in copies:
        copy.start()
    for copy in copies:
        copy.wait()


def body(features, tile_values, tile_rows, tile_cols, tile_count, weight, out_grad):
    n_row, n_col = lax.axis_size("row"), lax.axis_size("col")
    n_chip = n_row // 2
    nodes, width = features.shape
    slots, tile = tile_values.shape[2], tile_values.shape[3]
    tall, wide = n_col * nodes, n_row * nodes
    piece = 2 * width // n_row
    lanes = width // PARTS
    vmem, dma = pltpu.VMEM, pltpu.SemaphoreType.DMA
    anywhere = pl.BlockSpec(memory_space=pl.ANY)
    in_vmem = pl.BlockSpec(memory_space=pltpu.VMEM)
    scalars = pl.BlockSpec(memory_space=pltpu.SMEM)
    shapes = (
        jax.ShapeDtypeStruct((nodes, width), BF16),
        jax.ShapeDtypeStruct((nodes, width), BF16),
        jax.ShapeDtypeStruct((width, width), F32),
    )
    results = pl.pallas_call(
        functools.partial(kernel, n_row, n_col),
        out_shape=tuple(pltpu.VMEM(s.shape, s.dtype) for s in shapes),
        in_specs=[anywhere, anywhere, scalars, scalars, scalars, anywhere, anywhere],
        out_specs=(in_vmem,) * 3,
        scratch_shapes=[
            vmem((PARTS, wide, lanes), BF16),
            vmem((slots + 1, tile, tile), BF16),
            vmem((slots + 1, tile, tile), BF16),
            vmem((tall, wide), BF16),
            vmem((wide, tall), BF16),
            vmem((width, width), BF16),
            vmem((width, width), BF16),
            vmem((nodes, width), BF16),
            vmem((PARTS, tall, lanes), BF16),
            vmem((PARTS, n_col, nodes, lanes), BF16),
            vmem((PARTS, tall, lanes), BF16),
            vmem((PARTS, n_chip * nodes, lanes), BF16),
            vmem((PARTS, n_chip * nodes, lanes), BF16),
            vmem((PARTS, n_chip * nodes, lanes), BF16),
            vmem((PARTS, n_chip, nodes, lanes), BF16),
            vmem((2 * width, width // 2), BF16),
            vmem((n_row, piece, width // 2), BF16),
            vmem((n_col, piece, width // 2), BF16),
            vmem((2 * width, width // 2), BF16),
            pltpu.SMEM(((tall // tile) * (wide // tile),), jnp.int32),
            dma((3 + PARTS,)), dma((PARTS,)), dma((PARTS,)),
        ]
        + [dma((PARTS, n_chip))] * 4
        + [dma((PARTS, n_col))] * 4
        + [dma((PARTS,))] * 2 + [dma((PARTS, n_chip))] * 2
        + [dma((n_row,))] * 2 + [dma((n_col,))] * 2 + [dma((n_row,))] * 2,
        compiler_params=pltpu.CompilerParams(
            collective_id=0, has_side_effects=True, vmem_limit_bytes=56 * 1024 * 1024),
    )(features, tile_values[0, 0], tile_rows, tile_cols, tile_count, weight, out_grad)
    return tuple(pl.pallas_call(
        hand_over,
        out_shape=shapes,
        in_specs=[in_vmem] * 3,
        out_specs=(anywhere,) * 3,
        scratch_shapes=[dma((3,))],
    )(*(pltpu.with_memory_space_constraint(r, pltpu.VMEM) for r in results)))


def solution(mesh):
    placed = (
        P(("row", "col"), None),
        P("row", "col", None, None, None),
        P("row", "col", None),
        P("row", "col", None),
        P("row", "col"),
        P(),
        P(("row", "col"), None),
    )
    return jax.shard_map(
        body,
        mesh=mesh,
        in_specs=placed,
        out_specs=(P(("row", "col"), None), P(("row", "col"), None), P()),
        check_vma=False,
    )
```

```python
import functools

import jax
import jax.numpy as jnp
from jax import lax
from jax.experimental import pallas as pl
from jax.experimental.pallas import tpu as pltpu
from jax.sharding import PartitionSpec as P

MESH = pl.DeviceIdType.MESH
F32 = jnp.float32
BF16 = jnp.bfloat16


def repeat(low, high, step):
    if high - low <= 8:
        for k in range(low, high):
            step(k)
    else:

        def once(k, carry):
            step(k)
            return carry

        lax.fori_loop(low, high, once, 0)


def block(index, size):
    if isinstance(index, int):
        return pl.ds(index * size, size)
    return pl.ds(pl.multiple_of(index * size, size), size)


def partner(rank, k, size):
    assert size & (size - 1) == 0
    found, bit = 0, 1
    while bit < size:
        found = found + bit * ((rank // bit + k // bit) % 2)
        bit *= 2
    return found


def far_first(size, step):
    repeat(1, size, lambda m: step(size - m))


def dot(a, b):
    return jnp.dot(a, b, preferred_element_type=F32)


def gelu_and_slope(v):
    scale = 0.7978845608028654
    square = v * v
    t = jnp.tanh(scale * (v + 0.044715 * v * square))
    half = 0.5 * (1.0 + t)
    slope = half + 0.5 * v * (1.0 - t * t) * scale * (1.0 + 3 * 0.044715 * square)
    return v * half, slope


PARTS = 2


def kernel(
    n_row, n_col,
    feat_in, tiles_in, rows_ref, cols_ref, count_ref, weight_in, upstream_in,
    act, fgrad, wgrad,
    feat_all, tiles, tiles_t, adj, adj_t, weight, weight_t, upstream,
    part_send, part_recv, cot_all, sib_send, sib_recv, back_send, back_recv,
    w_send, w_recv, w_mid, w_all, slot_of,
    in_sem, sib_s, sib_r,
    feat_s, feat_r, fwd_s, fwd_r, part_s, part_r, cot_s, cot_r,
    pair_s, pair_r, back_s, back_r, w1_s, w1_r, w2_s, w2_r, w3_s, w3_r,
):
    i, j = lax.axis_index("row"), lax.axis_index("col")
    chip, core = i // 2, i % 2
    n_chip = n_row // 2
    sibling = 2 * chip + 1 - core
    nodes, width = feat_in.shape
    slots, tile = tiles_in.shape[0], tiles_in.shape[1]
    row_tiles = n_col * nodes // tile
    col_tiles = n_row * nodes // tile
    half = width // 2
    piece = 2 * width // n_row
    lanes = width // PARTS

    def to_row(src, dst, send, recv, peer):
        return pltpu.make_async_remote_copy(
            src_ref=src, dst_ref=dst, send_sem=send, recv_sem=recv,
            device_id=(peer, j), device_id_type=MESH)

    def to_col(src, dst, send, recv, peer):
        return pltpu.make_async_remote_copy(
            src_ref=src, dst_ref=dst, send_sem=send, recv_sem=recv,
            device_id=(i, peer), device_id_type=MESH)

    def row_peer(k):
        return partner(i, k, n_row)

    def col_peer(k):
        return partner(j, k, n_col)

    def mate(k):
        return 2 * partner(chip, k, n_chip) + core

    def strip(h):
        return pl.ds(h * lanes, lanes)

    loads = [
        pltpu.make_async_copy(tiles_in, tiles.at[pl.ds(0, slots)], in_sem.at[0]),
        pltpu.make_async_copy(weight_in, weight, in_sem.at[1]),
        pltpu.make_async_copy(upstream_in, upstream, in_sem.at[2]),
    ] + [
        pltpu.make_async_copy(feat_in.at[:, strip(h)], feat_all.at[h, block(i, nodes)],
                              in_sem.at[3 + h])
        for h in range(PARTS)
    ]
    for load in loads:
        load.start()

    barrier = pltpu.get_barrier_semaphore()
    repeat(1, n_row, lambda k: pl.semaphore_signal(
        barrier, inc=1, device_id=(row_peer(k), j), device_id_type=MESH))
    repeat(1, n_col, lambda k: pl.semaphore_signal(
        barrier, inc=1, device_id=(i, col_peer(k)), device_id_type=MESH))
    pl.semaphore_wait(barrier, n_row + n_col - 2)

    def feat_copy(h, k, owner):
        return to_row(feat_in.at[:, strip(h)], feat_all.at[h, block(owner, nodes)],
                      feat_s.at[h, k], feat_r.at[h, k], mate(k))

    def sib_copy(h, owner):
        return to_row(feat_in.at[:, strip(h)], feat_all.at[h, block(owner, nodes)],
                      sib_s.at[h], sib_r.at[h], sibling)

    def pass_copy(h, k, owner):
        place = feat_all.at[h, block(owner, nodes)]
        return to_row(place, place, fwd_s.at[h, k], fwd_r.at[h, k], sibling)

    for h in range(PARTS):
        far_first(n_chip, lambda k: feat_copy(h, k, i).start())
        sib_copy(h, i).start()

    count = count_ref[0, 0]
    places = [
        jnp.where(s < count, rows_ref[0, 0, s] * col_tiles + cols_ref[0, 0, s], -1)
        for s in range(slots)
    ]

    def find(spot):
        slot = jnp.int32(slots)
        for s, place in enumerate(places):
            slot = jnp.where(place == spot, jnp.int32(s), slot)
        slot_of[spot] = slot

    repeat(0, row_tiles, lambda r: repeat(0, col_tiles, lambda c: find(r * col_tiles + c)))
    tiles[slots] = jnp.zeros((tile, tile), BF16)
    tiles_t[slots] = jnp.zeros((tile, tile), BF16)
    loads[0].wait()

    def place_row(r):
        def place(c):
            adj[block(r, tile), block(c, tile)] = tiles[slot_of[r * col_tiles + c]]

        repeat(0, col_tiles, place)

    repeat(0, row_tiles, place_row)
    for load in loads[3:]:
        load.wait()

    last = PARTS - 1
    few = nodes // 2
    chunks = [(h, 0, nodes) for h in range(last)] + [(last, 0, few), (last, few, few)]

    def part_copy(n, k):
        h, first, size = chunks[n]
        rows = pl.ds(pl.multiple_of(col_peer(k) * nodes + first, few), size)
        return to_col(part_send.at[h, rows], part_recv.at[h, k, pl.ds(first, size)],
                      part_s.at[n, k], part_r.at[n, k], col_peer(k))

    for h in range(PARTS):

        def pass_on(k):
            feat_copy(h, k, mate(k)).wait_recv()
            pass_copy(h, k, mate(k)).start()

        far_first(n_chip, pass_on)
        sib_copy(h, sibling).wait_recv()
        far_first(n_chip, lambda k: pass_copy(h, k, mate(k) + sibling - i).wait_recv())

        part_send[h] = dot(adj[...], feat_all[h]).astype(BF16)
        for n, chunk in enumerate(chunks):
            if chunk[0] == h:
                far_first(n_col, lambda k: part_copy(n, k).start())
        part_recv[h, 0] = part_send[h, block(j, nodes), :]

    def flip(s):
        tiles_t[s] = tiles[s].T

    repeat(0, slots, flip)
    per = nodes // tile

    def place_back(r):
        def place(c):
            rank = c // per
            spot = ((rank % 2) * n_chip + rank // 2) * per + c % per
            adj_t[block(spot, tile), block(r, tile)] = tiles_t[slot_of[r * col_tiles + c]]

        repeat(0, col_tiles, place)

    repeat(0, row_tiles, place_back)
    loads[1].wait()
    loads[2].wait()
    weight_t[...] = weight[...].T
    for h in range(PARTS):

        def feat_sent(k):
            feat_copy(h, k, i).wait_send()
            pass_copy(h, k, mate(k)).wait_send()

        sib_copy(h, i).wait_send()
        repeat(1, n_chip, feat_sent)

    sendings = [(None, 0)] + [(h, few) for h in range(PARTS)]

    def cot_copy(n, k, owner):
        h, first = sendings[n]
        rows = pl.ds(pl.multiple_of(owner * nodes + first, few), few)
        place = cot_all.at[:, rows] if h is None else cot_all.at[h, rows]
        return to_col(place, place, cot_s.at[n, k], cot_r.at[n, k], col_peer(k))

    aggregates, cotangents = [], []
    for first in (0, few):
        rows = pl.ds(first, few)
        gathered = []
        preact = jnp.zeros((few, width), F32)
        for h in range(PARTS):
            for n, chunk in enumerate(chunks):
                if chunk[0] == h and (chunk[1] == first):
                    far_first(n_col, lambda k: part_copy(n, k).wait_recv())
            total = part_recv[h, 0, rows, :].astype(F32)
            for k in range(1, n_col):
                total = total + part_recv[h, k, rows, :].astype(F32)
            gathered.append(total.astype(BF16))
            preact = preact + dot(gathered[h], weight[strip(h), :])
        value, slope = gelu_and_slope(preact)
        cotangent = (upstream[rows, :].astype(F32) * slope).astype(BF16)
        for h in range(PARTS):
            spot = pl.ds(pl.multiple_of(j * nodes + first, few), few)
            cot_all[h, spot, :] = cotangent[:, h * lanes:(h + 1) * lanes]
        for n, sending in enumerate(sendings):
            if sending[1] == first:
                far_first(n_col, lambda k: cot_copy(n, k, j).start())
        act[rows, :] = value.astype(BF16)
        aggregates.append(jnp.concatenate(gathered, axis=1))
        cotangents.append(cotangent)
    aggregate = jnp.concatenate(aggregates, axis=0)
    cotangent = jnp.concatenate(cotangents, axis=0)

    term = lax.dot_general(aggregate, cotangent, (((0,), (0,)), ((), ())),
                           preferred_element_type=F32)
    term = (term * (nodes * n_row * n_col) ** -0.5).astype(BF16)
    w_send[pl.ds(0, width), :] = term[:, :half]
    w_send[pl.ds(width, width), :] = term[:, half:]

    def w1_copy(k):
        return to_row(w_send.at[block(row_peer(k), piece)], w_recv.at[k],
                      w1_s.at[k], w1_r.at[k], row_peer(k))

    far_first(n_row, lambda k: w1_copy(k).start())
    w_recv[0] = w_send[block(i, piece), :]
    for n in range(len(chunks)):
        repeat(1, n_col, lambda k: part_copy(n, k).wait_send())

    def w2_copy(k, owner):
        return to_col(w_mid.at[owner], w_mid.at[owner], w2_s.at[k], w2_r.at[k], col_peer(k))

    def w3_copy(k, owner):
        place = w_all.at[block(owner, piece)]
        return to_row(place, place, w3_s.at[k], w3_r.at[k], row_peer(k))

    def sum_over_row():
        far_first(n_row, lambda k: w1_copy(k).wait_recv())
        summed = w_recv[0].astype(F32)
        for k in range(1, n_row):
            summed = summed + w_recv[k].astype(F32)
        w_mid[j] = summed.astype(BF16)
        far_first(n_col, lambda k: w2_copy(k, j).start())

    def sum_over_col():
        far_first(n_col, lambda k: w2_copy(k, col_peer(k)).wait_recv())
        summed = w_mid[0].astype(F32)
        for k in range(1, n_col):
            summed = summed + w_mid[k].astype(F32)
        w_all[block(i, piece), :] = summed.astype(BF16)
        far_first(n_row, lambda k: w3_copy(k, i).start())

    def pair_copy(h):
        return to_row(sib_send.at[h], sib_recv.at[h], pair_s.at[h], pair_r.at[h], sibling)

    def back_copy(h, k):
        return to_row(back_send.at[h, block(partner(chip, k, n_chip), nodes)],
                      back_recv.at[h, k], back_s.at[h, k], back_r.at[h, k], mate(k))

    for h in range(PARTS):
        for n in (0, 1) if h == 0 else (h + 1,):
            far_first(n_col, lambda k: cot_copy(n, k, col_peer(k)).wait_recv())
        sib_send[h] = dot(adj_t[block(1 - core, n_chip * nodes), :], cot_all[h]).astype(BF16)
        pair_copy(h).start()
        mine = dot(adj_t[block(core, n_chip * nodes), :], cot_all[h])
        pair_copy(h).wait_recv()
        back_send[h] = (mine + sib_recv[h].astype(F32)).astype(BF16)
        far_first(n_chip, lambda k: back_copy(h, k).start())
        if h == 0:
            sum_over_row()
    sum_over_col()
    for h in range(PARTS):
        pair_copy(h).wait_send()
    for n in range(len(sendings)):
        repeat(1, n_col, lambda k: cot_copy(n, k, j).wait_send())
    repeat(1, n_row, lambda k: w1_copy(k).wait_send())
    repeat(1, n_col, lambda k: w2_copy(k, j).wait_send())

    grad = jnp.zeros((nodes, width), F32)
    for h in range(PARTS):
        far_first(n_chip, lambda k: back_copy(h, k).wait_recv())
        pulled = back_send[h, block(chip, nodes), :].astype(F32)
        for k in range(1, n_chip):
            pulled = pulled + back_recv[h, k].astype(F32)
        grad = grad + dot(pulled.astype(BF16), weight_t[strip(h), :])
    fgrad[...] = grad.astype(BF16)

    far_first(n_row, lambda k: w3_copy(k, row_peer(k)).wait_recv())
    wgrad[:, pl.ds(0, half)] = w_all[pl.ds(0, width), :].astype(F32)
    wgrad[:, pl.ds(half, half)] = w_all[pl.ds(width, width), :].astype(F32)

    repeat(1, n_row, lambda k: w3_copy(k, i).wait_send())
    for h in range(PARTS):
        repeat(1, n_chip, lambda k: back_copy(h, k).wait_send())


def hand_over(*refs):
    sources, results, sems = refs[:3], refs[3:6], refs[6]
    copies = [
        pltpu.make_async_copy(source, result, sems.at[n])
        for n, (source, result) in enumerate(zip(sources, results))
    ]
    for copy in copies:
        copy.start()
    for copy in copies:
        copy.wait()


def body(features, tile_values, tile_rows, tile_cols, tile_count, weight, out_grad):
    n_row, n_col = lax.axis_size("row"), lax.axis_size("col")
    n_chip = n_row // 2
    nodes, width = features.shape
    slots, tile = tile_values.shape[2], tile_values.shape[3]
    tall, wide = n_col * nodes, n_row * nodes
    piece = 2 * width // n_row
    lanes = width // PARTS
    vmem, dma = pltpu.VMEM, pltpu.SemaphoreType.DMA
    anywhere = pl.BlockSpec(memory_space=pl.ANY)
    in_vmem = pl.BlockSpec(memory_space=pltpu.VMEM)
    scalars = pl.BlockSpec(memory_space=pltpu.SMEM)
    shapes = (
        jax.ShapeDtypeStruct((nodes, width), BF16),
        jax.ShapeDtypeStruct((nodes, width), BF16),
        jax.ShapeDtypeStruct((width, width), F32),
    )
    results = pl.pallas_call(
        functools.partial(kernel, n_row, n_col),
        out_shape=tuple(pltpu.VMEM(s.shape, s.dtype) for s in shapes),
        in_specs=[anywhere, anywhere, scalars, scalars, scalars, anywhere, anywhere],
        out_specs=(in_vmem,) * 3,
        scratch_shapes=[
            vmem((PARTS, wide, lanes), BF16),
            vmem((slots + 1, tile, tile), BF16),
            vmem((slots + 1, tile, tile), BF16),
            vmem((tall, wide), BF16),
            vmem((wide, tall), BF16),
            vmem((width, width), BF16),
            vmem((width, width), BF16),
            vmem((nodes, width), BF16),
            vmem((PARTS, tall, lanes), BF16),
            vmem((PARTS, n_col, nodes, lanes), BF16),
            vmem((PARTS, tall, lanes), BF16),
            vmem((PARTS, n_chip * nodes, lanes), BF16),
            vmem((PARTS, n_chip * nodes, lanes), BF16),
            vmem((PARTS, n_chip * nodes, lanes), BF16),
            vmem((PARTS, n_chip, nodes, lanes), BF16),
            vmem((2 * width, width // 2), BF16),
            vmem((n_row, piece, width // 2), BF16),
            vmem((n_col, piece, width // 2), BF16),
            vmem((2 * width, width // 2), BF16),
            pltpu.SMEM(((tall // tile) * (wide // tile),), jnp.int32),
            dma((3 + PARTS,)), dma((PARTS,)), dma((PARTS,)),
        ]
        + [dma((PARTS, n_chip))] * 4
        + [dma((PARTS + 1, n_col))] * 4
        + [dma((PARTS,))] * 2 + [dma((PARTS, n_chip))] * 2
        + [dma((n_row,))] * 2 + [dma((n_col,))] * 2 + [dma((n_row,))] * 2,
        compiler_params=pltpu.CompilerParams(
            collective_id=0, has_side_effects=True, vmem_limit_bytes=56 * 1024 * 1024),
    )(features, tile_values[0, 0], tile_rows, tile_cols, tile_count, weight, out_grad)
    return tuple(pl.pallas_call(
        hand_over,
        out_shape=shapes,
        in_specs=[in_vmem] * 3,
        out_specs=(anywhere,) * 3,
        scratch_shapes=[dma((3,))],
    )(*(pltpu.with_memory_space_constraint(r, pltpu.VMEM) for r in results)))


def solution(mesh):
    placed = (
        P(("row", "col"), None),
        P("row", "col", None, None, None),
        P("row", "col", None),
        P("row", "col", None),
        P("row", "col"),
        P(),
        P(("row", "col"), None),
    )
    return jax.shard_map(
        body,
        mesh=mesh,
        in_specs=placed,
        out_specs=(P(("row", "col"), None), P(("row", "col"), None), P()),
        check_vma=False,
    )
```

```python
import functools

import jax
import jax.numpy as jnp
from jax import lax
from jax.experimental import pallas as pl
from jax.experimental.pallas import tpu as pltpu
from jax.sharding import PartitionSpec as P

MESH = pl.DeviceIdType.MESH
F32 = jnp.float32
BF16 = jnp.bfloat16


def repeat(low, high, step):
    if high - low <= 8:
        for k in range(low, high):
            step(k)
    else:

        def once(k, carry):
            step(k)
            return carry

        lax.fori_loop(low, high, once, 0)


def block(index, size):
    if isinstance(index, int):
        return pl.ds(index * size, size)
    return pl.ds(pl.multiple_of(index * size, size), size)


def partner(rank, k, size):
    assert size & (size - 1) == 0
    found, bit = 0, 1
    while bit < size:
        found = found + bit * ((rank // bit + k // bit) % 2)
        bit *= 2
    return found


def far_first(size, step):
    repeat(1, size, lambda m: step(size - m))


def dot(a, b):
    return jnp.dot(a, b, preferred_element_type=F32)


def gelu_and_slope(v):
    scale = 0.7978845608028654
    square = v * v
    t = jnp.tanh(scale * (v + 0.044715 * v * square))
    half = 0.5 * (1.0 + t)
    slope = half + 0.5 * v * (1.0 - t * t) * scale * (1.0 + 3 * 0.044715 * square)
    return v * half, slope


PARTS = 2


def kernel(
    n_row, n_col,
    feat_in, tiles_in, rows_ref, cols_ref, count_ref, weight_in, upstream_in,
    act, fgrad, wgrad,
    feat_all, tiles, tiles_t, adj, adj_t, weight, weight_t, upstream,
    part_send, part_recv, cot_all, sib_send, sib_recv, back_send, back_recv,
    w_send, w_recv, w_mid, w_all, slot_of,
    in_sem, sib_s, sib_r,
    feat_s, feat_r, fwd_s, fwd_r, part_s, part_r, cot_s, cot_r,
    pair_s, pair_r, back_s, back_r, w1_s, w1_r, w2_s, w2_r, w3_s, w3_r,
):
    i, j = lax.axis_index("row"), lax.axis_index("col")
    chip, core = i // 2, i % 2
    n_chip = n_row // 2
    sibling = 2 * chip + 1 - core
    nodes, width = feat_in.shape
    slots, tile = tiles_in.shape[0], tiles_in.shape[1]
    row_tiles = n_col * nodes // tile
    col_tiles = n_row * nodes // tile
    half = width // 2
    piece = 2 * width // n_row
    lanes = width // PARTS

    def to_row(src, dst, send, recv, peer):
        return pltpu.make_async_remote_copy(
            src_ref=src, dst_ref=dst, send_sem=send, recv_sem=recv,
            device_id=(peer, j), device_id_type=MESH)

    def to_col(src, dst, send, recv, peer):
        return pltpu.make_async_remote_copy(
            src_ref=src, dst_ref=dst, send_sem=send, recv_sem=recv,
            device_id=(i, peer), device_id_type=MESH)

    def row_peer(k):
        return partner(i, k, n_row)

    def col_peer(k):
        return partner(j, k, n_col)

    def mate(k):
        return 2 * partner(chip, k, n_chip) + core

    def strip(h):
        return pl.ds(h * lanes, lanes)

    loads = [
        pltpu.make_async_copy(tiles_in, tiles.at[pl.ds(0, slots)], in_sem.at[0]),
        pltpu.make_async_copy(weight_in, weight, in_sem.at[1]),
        pltpu.make_async_copy(upstream_in, upstream, in_sem.at[2]),
    ] + [
        pltpu.make_async_copy(feat_in.at[:, strip(h)], feat_all.at[h, block(i, nodes)],
                              in_sem.at[3 + h])
        for h in range(PARTS)
    ]
    for load in loads:
        load.start()

    barrier = pltpu.get_barrier_semaphore()
    repeat(1, n_row, lambda k: pl.semaphore_signal(
        barrier, inc=1, device_id=(row_peer(k), j), device_id_type=MESH))
    repeat(1, n_col, lambda k: pl.semaphore_signal(
        barrier, inc=1, device_id=(i, col_peer(k)), device_id_type=MESH))
    count = count_ref[0, 0]
    places = [
        jnp.where(s < count, rows_ref[0, 0, s] * col_tiles + cols_ref[0, 0, s], -1)
        for s in range(slots)
    ]

    def find(spot):
        slot = jnp.int32(slots)
        for s, place in enumerate(places):
            slot = jnp.where(place == spot, jnp.int32(s), slot)
        slot_of[spot] = slot

    repeat(0, row_tiles, lambda r: repeat(0, col_tiles, lambda c: find(r * col_tiles + c)))
    tiles[slots] = jnp.zeros((tile, tile), BF16)
    tiles_t[slots] = jnp.zeros((tile, tile), BF16)
    pl.semaphore_wait(barrier, n_row + n_col - 2)

    def feat_copy(h, k, owner):
        return to_row(feat_in.at[:, strip(h)], feat_all.at[h, block(owner, nodes)],
                      feat_s.at[h, k], feat_r.at[h, k], mate(k))

    def sib_copy(h, owner):
        return to_row(feat_in.at[:, strip(h)], feat_all.at[h, block(owner, nodes)],
                      sib_s.at[h], sib_r.at[h], sibling)

    def pass_copy(h, k, owner):
        place = feat_all.at[h, block(owner, nodes)]
        return to_row(place, place, fwd_s.at[h, k], fwd_r.at[h, k], sibling)

    for h in range(PARTS):
        far_first(n_chip, lambda k: feat_copy(h, k, i).start())
        sib_copy(h, i).start()

    loads[0].wait()

    def place_row(r):
        def place(c):
            adj[block(r, tile), block(c, tile)] = tiles[slot_of[r * col_tiles + c]]

        repeat(0, col_tiles, place)

    repeat(0, row_tiles, place_row)
    for load in loads[3:]:
        load.wait()

    def part_copy(h, k):
        return to_col(part_send.at[h, block(col_peer(k), nodes)], part_recv.at[h, k],
                      part_s.at[h, k], part_r.at[h, k], col_peer(k))

    for h in range(PARTS):

        def pass_on(k):
            feat_copy(h, k, mate(k)).wait_recv()
            pass_copy(h, k, mate(k)).start()

        far_first(n_chip, pass_on)
        sib_copy(h, sibling).wait_recv()
        far_first(n_chip, lambda k: pass_copy(h, k, mate(k) + sibling - i).wait_recv())

        part_send[h] = dot(adj[...], feat_all[h]).astype(BF16)
        far_first(n_col, lambda k: part_copy(h, k).start())
        part_recv[h, 0] = part_send[h, block(j, nodes), :]

    def flip(s):
        tiles_t[s] = tiles[s].T

    repeat(0, slots, flip)
    per = nodes // tile

    def place_back(r):
        def place(c):
            rank = c // per
            spot = ((rank % 2) * n_chip + rank // 2) * per + c % per
            adj_t[block(spot, tile), block(r, tile)] = tiles_t[slot_of[r * col_tiles + c]]

        repeat(0, col_tiles, place)

    repeat(0, row_tiles, place_back)
    loads[1].wait()
    loads[2].wait()
    weight_t[...] = weight[...].T
    for h in range(PARTS):

        def feat_sent(k):
            feat_copy(h, k, i).wait_send()
            pass_copy(h, k, mate(k)).wait_send()

        sib_copy(h, i).wait_send()
        repeat(1, n_chip, feat_sent)

    gathered = []
    preact = jnp.zeros((nodes, width), F32)
    for h in range(PARTS):
        far_first(n_col, lambda k: part_copy(h, k).wait_recv())
        total = part_recv[h, 0].astype(F32)
        for k in range(1, n_col):
            total = total + part_recv[h, k].astype(F32)
        gathered.append(total.astype(BF16))
        preact = preact + dot(gathered[h], weight[strip(h), :])
    aggregate = jnp.concatenate(gathered, axis=1)
    value, slope = gelu_and_slope(preact)
    cotangent = (upstream[...].astype(F32) * slope).astype(BF16)

    def cot_copy(h, k, owner):
        place = cot_all.at[h, block(owner, nodes)]
        return to_col(place, place, cot_s.at[h, k], cot_r.at[h, k], col_peer(k))

    for h in range(PARTS):
        cot_all[h, block(j, nodes), :] = cotangent[:, h * lanes:(h + 1) * lanes]
        far_first(n_col, lambda k: cot_copy(h, k, j).start())
    act[...] = value.astype(BF16)

    term = lax.dot_general(aggregate, cotangent, (((0,), (0,)), ((), ())),
                           preferred_element_type=F32)
    term = (term * (nodes * n_row * n_col) ** -0.5).astype(BF16)
    w_send[pl.ds(0, width), :] = term[:, :half]
    w_send[pl.ds(width, width), :] = term[:, half:]

    def w1_copy(k):
        return to_row(w_send.at[block(row_peer(k), piece)], w_recv.at[k],
                      w1_s.at[k], w1_r.at[k], row_peer(k))

    far_first(n_row, lambda k: w1_copy(k).start())
    w_recv[0] = w_send[block(i, piece), :]
    for h in range(PARTS):
        repeat(1, n_col, lambda k: part_copy(h, k).wait_send())

    def w2_copy(k, owner):
        return to_col(w_mid.at[owner], w_mid.at[owner], w2_s.at[k], w2_r.at[k], col_peer(k))

    def w3_copy(k, owner):
        place = w_all.at[block(owner, piece)]
        return to_row(place, place, w3_s.at[k], w3_r.at[k], row_peer(k))

    def sum_over_row():
        far_first(n_row, lambda k: w1_copy(k).wait_recv())
        summed = w_recv[0].astype(F32)
        for k in range(1, n_row):
            summed = summed + w_recv[k].astype(F32)
        w_mid[j] = summed.astype(BF16)
        far_first(n_col, lambda k: w2_copy(k, j).start())

    def sum_over_col():
        far_first(n_col, lambda k: w2_copy(k, col_peer(k)).wait_recv())
        summed = w_mid[0].astype(F32)
        for k in range(1, n_col):
            summed = summed + w_mid[k].astype(F32)
        w_all[block(i, piece), :] = summed.astype(BF16)
        far_first(n_row, lambda k: w3_copy(k, i).start())

    def pair_copy(h):
        return to_row(sib_send.at[h], sib_recv.at[h], pair_s.at[h], pair_r.at[h], sibling)

    def back_copy(h, k):
        return to_row(back_send.at[h, block(partner(chip, k, n_chip), nodes)],
                      back_recv.at[h, k], back_s.at[h, k], back_r.at[h, k], mate(k))

    for h in range(PARTS):
        far_first(n_col, lambda k: cot_copy(h, k, col_peer(k)).wait_recv())
        sib_send[h] = dot(adj_t[block(1 - core, n_chip * nodes), :], cot_all[h]).astype(BF16)
        pair_copy(h).start()
    for h in range(PARTS):
        mine = dot(adj_t[block(core, n_chip * nodes), :], cot_all[h])
        pair_copy(h).wait_recv()
        back_send[h] = (mine + sib_recv[h].astype(F32)).astype(BF16)
        far_first(n_chip, lambda k: back_copy(h, k).start())
        if h == 0:
            sum_over_row()
    sum_over_col()
    for h in range(PARTS):
        pair_copy(h).wait_send()
        repeat(1, n_col, lambda k: cot_copy(h, k, j).wait_send())
    repeat(1, n_row, lambda k: w1_copy(k).wait_send())
    repeat(1, n_col, lambda k: w2_copy(k, j).wait_send())

    grad = jnp.zeros((nodes, width), F32)
    for h in range(PARTS):
        far_first(n_chip, lambda k: back_copy(h, k).wait_recv())
        pulled = back_send[h, block(chip, nodes), :].astype(F32)
        for k in range(1, n_chip):
            pulled = pulled + back_recv[h, k].astype(F32)
        grad = grad + dot(pulled.astype(BF16), weight_t[strip(h), :])
    fgrad[...] = grad.astype(BF16)

    far_first(n_row, lambda k: w3_copy(k, row_peer(k)).wait_recv())
    wgrad[:, pl.ds(0, half)] = w_all[pl.ds(0, width), :].astype(F32)
    wgrad[:, pl.ds(half, half)] = w_all[pl.ds(width, width), :].astype(F32)

    repeat(1, n_row, lambda k: w3_copy(k, i).wait_send())
    for h in range(PARTS):
        repeat(1, n_chip, lambda k: back_copy(h, k).wait_send())


def hand_over(*refs):
    sources, results, sems = refs[:3], refs[3:6], refs[6]
    copies = [
        pltpu.make_async_copy(source, result, sems.at[n])
        for n, (source, result) in enumerate(zip(sources, results))
    ]
    for copy in copies:
        copy.start()
    for copy in copies:
        copy.wait()


def body(features, tile_values, tile_rows, tile_cols, tile_count, weight, out_grad):
    n_row, n_col = lax.axis_size("row"), lax.axis_size("col")
    n_chip = n_row // 2
    nodes, width = features.shape
    slots, tile = tile_values.shape[2], tile_values.shape[3]
    tall, wide = n_col * nodes, n_row * nodes
    piece = 2 * width // n_row
    lanes = width // PARTS
    vmem, dma = pltpu.VMEM, pltpu.SemaphoreType.DMA
    anywhere = pl.BlockSpec(memory_space=pl.ANY)
    in_vmem = pl.BlockSpec(memory_space=pltpu.VMEM)
    scalars = pl.BlockSpec(memory_space=pltpu.SMEM)
    shapes = (
        jax.ShapeDtypeStruct((nodes, width), BF16),
        jax.ShapeDtypeStruct((nodes, width), BF16),
        jax.ShapeDtypeStruct((width, width), F32),
    )
    results = pl.pallas_call(
        functools.partial(kernel, n_row, n_col),
        out_shape=tuple(pltpu.VMEM(s.shape, s.dtype) for s in shapes),
        in_specs=[anywhere, anywhere, scalars, scalars, scalars, anywhere, anywhere],
        out_specs=(in_vmem,) * 3,
        scratch_shapes=[
            vmem((PARTS, wide, lanes), BF16),
            vmem((slots + 1, tile, tile), BF16),
            vmem((slots + 1, tile, tile), BF16),
            vmem((tall, wide), BF16),
            vmem((wide, tall), BF16),
            vmem((width, width), BF16),
            vmem((width, width), BF16),
            vmem((nodes, width), BF16),
            vmem((PARTS, tall, lanes), BF16),
            vmem((PARTS, n_col, nodes, lanes), BF16),
            vmem((PARTS, tall, lanes), BF16),
            vmem((PARTS, n_chip * nodes, lanes), BF16),
            vmem((PARTS, n_chip * nodes, lanes), BF16),
            vmem((PARTS, n_chip * nodes, lanes), BF16),
            vmem((PARTS, n_chip, nodes, lanes), BF16),
            vmem((2 * width, width // 2), BF16),
            vmem((n_row, piece, width // 2), BF16),
            vmem((n_col, piece, width // 2), BF16),
            vmem((2 * width, width // 2), BF16),
            pltpu.SMEM(((tall // tile) * (wide // tile),), jnp.int32),
            dma((3 + PARTS,)), dma((PARTS,)), dma((PARTS,)),
        ]
        + [dma((PARTS, n_chip))] * 4
        + [dma((PARTS, n_col))] * 4
        + [dma((PARTS,))] * 2 + [dma((PARTS, n_chip))] * 2
        + [dma((n_row,))] * 2 + [dma((n_col,))] * 2 + [dma((n_row,))] * 2,
        compiler_params=pltpu.CompilerParams(
            collective_id=0, has_side_effects=True, vmem_limit_bytes=56 * 1024 * 1024),
    )(features, tile_values[0, 0], tile_rows, tile_cols, tile_count, weight, out_grad)
    return tuple(pl.pallas_call(
        hand_over,
        out_shape=shapes,
        in_specs=[in_vmem] * 3,
        out_specs=(anywhere,) * 3,
        scratch_shapes=[dma((3,))],
    )(*(pltpu.with_memory_space_constraint(r, pltpu.VMEM) for r in results)))


def solution(mesh):
    placed = (
        P(("row", "col"), None),
        P("row", "col", None, None, None),
        P("row", "col", None),
        P("row", "col", None),
        P("row", "col"),
        P(),
        P(("row", "col"), None),
    )
    return jax.shard_map(
        body,
        mesh=mesh,
        in_specs=placed,
        out_specs=(P(("row", "col"), None), P(("row", "col"), None), P()),
        check_vma=False,
    )
```

```python
import functools

import jax
import jax.numpy as jnp
from jax import lax
from jax.experimental import pallas as pl
from jax.experimental.pallas import tpu as pltpu
from jax.sharding import PartitionSpec as P

MESH = pl.DeviceIdType.MESH
F32 = jnp.float32
BF16 = jnp.bfloat16


def repeat(low, high, step):
    if high - low <= 8:
        for k in range(low, high):
            step(k)
    else:

        def once(k, carry):
            step(k)
            return carry

        lax.fori_loop(low, high, once, 0)


def block(index, size):
    if isinstance(index, int):
        return pl.ds(index * size, size)
    return pl.ds(pl.multiple_of(index * size, size), size)


def partner(rank, k, size):
    assert size & (size - 1) == 0
    found, bit = 0, 1
    while bit < size:
        found = found + bit * ((rank // bit + k // bit) % 2)
        bit *= 2
    return found


def far_first(size, step):
    repeat(1, size, lambda m: step(size - m))


def dot(a, b):
    return jnp.dot(a, b, preferred_element_type=F32)


def gelu_and_slope(v):
    scale = 0.7978845608028654
    square = v * v
    t = jnp.tanh(scale * (v + 0.044715 * v * square))
    half = 0.5 * (1.0 + t)
    slope = half + 0.5 * v * (1.0 - t * t) * scale * (1.0 + 3 * 0.044715 * square)
    return v * half, slope


PARTS = 2


def kernel(
    n_row, n_col,
    feat_in, tiles_in, rows_ref, cols_ref, count_ref, weight_in, upstream_in,
    act, fgrad, wgrad,
    feat_all, tiles, tiles_t, adj, adj_t, weight, weight_t, upstream,
    part_send, part_recv, cot_all, sib_send, sib_recv, back_send, back_recv,
    w_send, w_recv, w_mid, w_all, slot_of,
    in_sem, sib_s, sib_r,
    feat_s, feat_r, fwd_s, fwd_r, part_s, part_r, cot_s, cot_r,
    pair_s, pair_r, back_s, back_r, w1_s, w1_r, w2_s, w2_r, w3_s, w3_r,
):
    i, j = lax.axis_index("row"), lax.axis_index("col")
    chip, core = i // 2, i % 2
    n_chip = n_row // 2
    sibling = 2 * chip + 1 - core
    nodes, width = feat_in.shape
    slots, tile = tiles_in.shape[0], tiles_in.shape[1]
    row_tiles = n_col * nodes // tile
    col_tiles = n_row * nodes // tile
    half = width // 2
    piece = 2 * width // n_row
    lanes = width // PARTS

    def to_row(src, dst, send, recv, peer):
        return pltpu.make_async_remote_copy(
            src_ref=src, dst_ref=dst, send_sem=send, recv_sem=recv,
            device_id=(peer, j), device_id_type=MESH)

    def to_col(src, dst, send, recv, peer):
        return pltpu.make_async_remote_copy(
            src_ref=src, dst_ref=dst, send_sem=send, recv_sem=recv,
            device_id=(i, peer), device_id_type=MESH)

    def row_peer(k):
        return partner(i, k, n_row)

    def col_peer(k):
        return partner(j, k, n_col)

    def mate(k):
        return 2 * partner(chip, k, n_chip) + core

    def strip(h):
        return pl.ds(h * lanes, lanes)

    loads = [
        pltpu.make_async_copy(tiles_in, tiles.at[pl.ds(0, slots)], in_sem.at[0]),
        pltpu.make_async_copy(weight_in, weight, in_sem.at[1]),
        pltpu.make_async_copy(upstream_in, upstream, in_sem.at[2]),
    ] + [
        pltpu.make_async_copy(feat_in.at[:, strip(h)], feat_all.at[h, block(i, nodes)],
                              in_sem.at[3 + h])
        for h in range(PARTS)
    ]
    for load in loads:
        load.start()

    barrier = pltpu.get_barrier_semaphore()
    repeat(1, n_row, lambda k: pl.semaphore_signal(
        barrier, inc=1, device_id=(row_peer(k), j), device_id_type=MESH))
    repeat(1, n_col, lambda k: pl.semaphore_signal(
        barrier, inc=1, device_id=(i, col_peer(k)), device_id_type=MESH))
    pl.semaphore_wait(barrier, n_row + n_col - 2)

    def feat_copy(h, k, owner):
        return to_row(feat_in.at[:, strip(h)], feat_all.at[h, block(owner, nodes)],
                      feat_s.at[h, k], feat_r.at[h, k], mate(k))

    def sib_copy(h, owner):
        return to_row(feat_in.at[:, strip(h)], feat_all.at[h, block(owner, nodes)],
                      sib_s.at[h], sib_r.at[h], sibling)

    def pass_copy(h, k, owner):
        place = feat_all.at[h, block(owner, nodes)]
        return to_row(place, place, fwd_s.at[h, k], fwd_r.at[h, k], sibling)

    for h in range(PARTS):
        far_first(n_chip, lambda k: feat_copy(h, k, i).start())
        sib_copy(h, i).start()

    count = count_ref[0, 0]
    places = [
        jnp.where(s < count, rows_ref[0, 0, s] * col_tiles + cols_ref[0, 0, s], -1)
        for s in range(slots)
    ]

    def find(spot):
        slot = jnp.int32(slots)
        for s, place in enumerate(places):
            slot = jnp.where(place == spot, jnp.int32(s), slot)
        slot_of[spot] = slot

    repeat(0, row_tiles, lambda r: repeat(0, col_tiles, lambda c: find(r * col_tiles + c)))
    tiles[slots] = jnp.zeros((tile, tile), BF16)
    tiles_t[slots] = jnp.zeros((tile, tile), BF16)
    loads[0].wait()

    def place_row(r):
        def place(c):
            adj[block(r, tile), block(c, tile)] = tiles[slot_of[r * col_tiles + c]]

        repeat(0, col_tiles, place)

    repeat(0, row_tiles, place_row)
    for load in loads[3:]:
        load.wait()

    last = PARTS - 1
    few = nodes // 2
    chunks = [(h, 0, nodes) for h in range(last)] + [(last, 0, few), (last, few, few)]

    def part_copy(n, k):
        h, first, size = chunks[n]
        rows = pl.ds(pl.multiple_of(col_peer(k) * nodes + first, few), size)
        return to_col(part_send.at[h, rows], part_recv.at[h, k, pl.ds(first, size)],
                      part_s.at[n, k], part_r.at[n, k], col_peer(k))

    for h in range(PARTS):

        def pass_on(k):
            feat_copy(h, k, mate(k)).wait_recv()
            pass_copy(h, k, mate(k)).start()

        far_first(n_chip, pass_on)
        sib_copy(h, sibling).wait_recv()
        far_first(n_chip, lambda k: pass_copy(h, k, mate(k) + sibling - i).wait_recv())

        part_send[h] = dot(adj[...], feat_all[h]).astype(BF16)
        for n, chunk in enumerate(chunks):
            if chunk[0] == h:
                far_first(n_col, lambda k: part_copy(n, k).start())
        part_recv[h, 0] = part_send[h, block(j, nodes), :]

    def flip(s):
        tiles_t[s] = tiles[s].T

    repeat(0, slots, flip)
    per = nodes // tile

    def place_back(r):
        def place(c):
            rank = c // per
            spot = ((rank % 2) * n_chip + rank // 2) * per + c % per
            adj_t[block(spot, tile), block(r, tile)] = tiles_t[slot_of[r * col_tiles + c]]

        repeat(0, col_tiles, place)

    repeat(0, row_tiles, place_back)
    loads[1].wait()
    loads[2].wait()
    weight_t[...] = weight[...].T
    for h in range(PARTS):

        def feat_sent(k):
            feat_copy(h, k, i).wait_send()
            pass_copy(h, k, mate(k)).wait_send()

        sib_copy(h, i).wait_send()
        repeat(1, n_chip, feat_sent)

    sendings = [(0, 0, few), (0, few, few)] + [(h, 0, nodes) for h in range(1, PARTS)]

    def cot_copy(n, k, owner):
        h, first, size = sendings[n]
        place = cot_all.at[h, pl.ds(pl.multiple_of(owner * nodes + first, few), size)]
        return to_col(place, place, cot_s.at[n, k], cot_r.at[n, k], col_peer(k))

    aggregates, cotangents = [], []
    for first in (0, few):
        rows = pl.ds(first, few)
        gathered = []
        preact = jnp.zeros((few, width), F32)
        for h in range(PARTS):
            for n, chunk in enumerate(chunks):
                if chunk[0] == h and (chunk[1] == first):
                    far_first(n_col, lambda k: part_copy(n, k).wait_recv())
            total = part_recv[h, 0, rows, :].astype(F32)
            for k in range(1, n_col):
                total = total + part_recv[h, k, rows, :].astype(F32)
            gathered.append(total.astype(BF16))
            preact = preact + dot(gathered[h], weight[strip(h), :])
        value, slope = gelu_and_slope(preact)
        cotangent = (upstream[rows, :].astype(F32) * slope).astype(BF16)
        for h in range(PARTS):
            spot = pl.ds(pl.multiple_of(j * nodes + first, few), few)
            cot_all[h, spot, :] = cotangent[:, h * lanes:(h + 1) * lanes]
        for n in range(len(sendings)):
            if (n == 0) == (first == 0):
                far_first(n_col, lambda k: cot_copy(n, k, j).start())
        act[rows, :] = value.astype(BF16)
        aggregates.append(jnp.concatenate(gathered, axis=1))
        cotangents.append(cotangent)
    aggregate = jnp.concatenate(aggregates, axis=0)
    cotangent = jnp.concatenate(cotangents, axis=0)

    term = lax.dot_general(aggregate, cotangent, (((0,), (0,)), ((), ())),
                           preferred_element_type=F32)
    term = (term * (nodes * n_row * n_col) ** -0.5).astype(BF16)
    w_send[pl.ds(0, width), :] = term[:, :half]
    w_send[pl.ds(width, width), :] = term[:, half:]

    def w1_copy(k):
        return to_row(w_send.at[block(row_peer(k), piece)], w_recv.at[k],
                      w1_s.at[k], w1_r.at[k], row_peer(k))

    far_first(n_row, lambda k: w1_copy(k).start())
    w_recv[0] = w_send[block(i, piece), :]
    for n in range(len(chunks)):
        repeat(1, n_col, lambda k: part_copy(n, k).wait_send())

    def w2_copy(k, owner):
        return to_col(w_mid.at[owner], w_mid.at[owner], w2_s.at[k], w2_r.at[k], col_peer(k))

    def w3_copy(k, owner):
        place = w_all.at[block(owner, piece)]
        return to_row(place, place, w3_s.at[k], w3_r.at[k], row_peer(k))

    def sum_over_row():
        far_first(n_row, lambda k: w1_copy(k).wait_recv())
        summed = w_recv[0].astype(F32)
        for k in range(1, n_row):
            summed = summed + w_recv[k].astype(F32)
        w_mid[j] = summed.astype(BF16)
        far_first(n_col, lambda k: w2_copy(k, j).start())

    def sum_over_col():
        far_first(n_col, lambda k: w2_copy(k, col_peer(k)).wait_recv())
        summed = w_mid[0].astype(F32)
        for k in range(1, n_col):
            summed = summed + w_mid[k].astype(F32)
        w_all[block(i, piece), :] = summed.astype(BF16)
        far_first(n_row, lambda k: w3_copy(k, i).start())

    def pair_copy(h):
        return to_row(sib_send.at[h], sib_recv.at[h], pair_s.at[h], pair_r.at[h], sibling)

    def back_copy(h, k):
        return to_row(back_send.at[h, block(partner(chip, k, n_chip), nodes)],
                      back_recv.at[h, k], back_s.at[h, k], back_r.at[h, k], mate(k))

    for h in range(PARTS):
        for n in (0, 1) if h == 0 else (h + 1,):
            far_first(n_col, lambda k: cot_copy(n, k, col_peer(k)).wait_recv())
        sib_send[h] = dot(adj_t[block(1 - core, n_chip * nodes), :], cot_all[h]).astype(BF16)
        pair_copy(h).start()
        mine = dot(adj_t[block(core, n_chip * nodes), :], cot_all[h])
        pair_copy(h).wait_recv()
        back_send[h] = (mine + sib_recv[h].astype(F32)).astype(BF16)
        far_first(n_chip, lambda k: back_copy(h, k).start())
        if h == 0:
            sum_over_row()
    sum_over_col()
    for h in range(PARTS):
        pair_copy(h).wait_send()
    for n in range(len(sendings)):
        repeat(1, n_col, lambda k: cot_copy(n, k, j).wait_send())
    repeat(1, n_row, lambda k: w1_copy(k).wait_send())
    repeat(1, n_col, lambda k: w2_copy(k, j).wait_send())

    grad = jnp.zeros((nodes, width), F32)
    for h in range(PARTS):
        far_first(n_chip, lambda k: back_copy(h, k).wait_recv())
        pulled = back_send[h, block(chip, nodes), :].astype(F32)
        for k in range(1, n_chip):
            pulled = pulled + back_recv[h, k].astype(F32)
        grad = grad + dot(pulled.astype(BF16), weight_t[strip(h), :])
    fgrad[...] = grad.astype(BF16)

    far_first(n_row, lambda k: w3_copy(k, row_peer(k)).wait_recv())
    wgrad[:, pl.ds(0, half)] = w_all[pl.ds(0, width), :].astype(F32)
    wgrad[:, pl.ds(half, half)] = w_all[pl.ds(width, width), :].astype(F32)

    repeat(1, n_row, lambda k: w3_copy(k, i).wait_send())
    for h in range(PARTS):
        repeat(1, n_chip, lambda k: back_copy(h, k).wait_send())


def hand_over(*refs):
    sources, results, sems = refs[:3], refs[3:6], refs[6]
    copies = [
        pltpu.make_async_copy(source, result, sems.at[n])
        for n, (source, result) in enumerate(zip(sources, results))
    ]
    for copy in copies:
        copy.start()
    for copy in copies:
        copy.wait()


def body(features, tile_values, tile_rows, tile_cols, tile_count, weight, out_grad):
    n_row, n_col = lax.axis_size("row"), lax.axis_size("col")
    n_chip = n_row // 2
    nodes, width = features.shape
    slots, tile = tile_values.shape[2], tile_values.shape[3]
    tall, wide = n_col * nodes, n_row * nodes
    piece = 2 * width // n_row
    lanes = width // PARTS
    vmem, dma = pltpu.VMEM, pltpu.SemaphoreType.DMA
    anywhere = pl.BlockSpec(memory_space=pl.ANY)
    in_vmem = pl.BlockSpec(memory_space=pltpu.VMEM)
    scalars = pl.BlockSpec(memory_space=pltpu.SMEM)
    shapes = (
        jax.ShapeDtypeStruct((nodes, width), BF16),
        jax.ShapeDtypeStruct((nodes, width), BF16),
        jax.ShapeDtypeStruct((width, width), F32),
    )
    results = pl.pallas_call(
        functools.partial(kernel, n_row, n_col),
        out_shape=tuple(pltpu.VMEM(s.shape, s.dtype) for s in shapes),
        in_specs=[anywhere, anywhere, scalars, scalars, scalars, anywhere, anywhere],
        out_specs=(in_vmem,) * 3,
        scratch_shapes=[
            vmem((PARTS, wide, lanes), BF16),
            vmem((slots + 1, tile, tile), BF16),
            vmem((slots + 1, tile, tile), BF16),
            vmem((tall, wide), BF16),
            vmem((wide, tall), BF16),
            vmem((width, width), BF16),
            vmem((width, width), BF16),
            vmem((nodes, width), BF16),
            vmem((PARTS, tall, lanes), BF16),
            vmem((PARTS, n_col, nodes, lanes), BF16),
            vmem((PARTS, tall, lanes), BF16),
            vmem((PARTS, n_chip * nodes, lanes), BF16),
            vmem((PARTS, n_chip * nodes, lanes), BF16),
            vmem((PARTS, n_chip * nodes, lanes), BF16),
            vmem((PARTS, n_chip, nodes, lanes), BF16),
            vmem((2 * width, width // 2), BF16),
            vmem((n_row, piece, width // 2), BF16),
            vmem((n_col, piece, width // 2), BF16),
            vmem((2 * width, width // 2), BF16),
            pltpu.SMEM(((tall // tile) * (wide // tile),), jnp.int32),
            dma((3 + PARTS,)), dma((PARTS,)), dma((PARTS,)),
        ]
        + [dma((PARTS, n_chip))] * 4
        + [dma((PARTS + 1, n_col))] * 4
        + [dma((PARTS,))] * 2 + [dma((PARTS, n_chip))] * 2
        + [dma((n_row,))] * 2 + [dma((n_col,))] * 2 + [dma((n_row,))] * 2,
        compiler_params=pltpu.CompilerParams(
            collective_id=0, has_side_effects=True, vmem_limit_bytes=56 * 1024 * 1024),
    )(features, tile_values[0, 0], tile_rows, tile_cols, tile_count, weight, out_grad)
    return tuple(pl.pallas_call(
        hand_over,
        out_shape=shapes,
        in_specs=[in_vmem] * 3,
        out_specs=(anywhere,) * 3,
        scratch_shapes=[dma((3,))],
    )(*(pltpu.with_memory_space_constraint(r, pltpu.VMEM) for r in results)))


def solution(mesh):
    placed = (
        P(("row", "col"), None),
        P("row", "col", None, None, None),
        P("row", "col", None),
        P("row", "col", None),
        P("row", "col"),
        P(),
        P(("row", "col"), None),
    )
    return jax.shard_map(
        body,
        mesh=mesh,
        in_specs=placed,
        out_specs=(P(("row", "col"), None), P(("row", "col"), None), P()),
        check_vma=False,
    )
```

```python
import functools

import jax
import jax.numpy as jnp
from jax import lax
from jax.experimental import pallas as pl
from jax.experimental.pallas import tpu as pltpu
from jax.sharding import PartitionSpec as P

MESH = pl.DeviceIdType.MESH
F32 = jnp.float32
BF16 = jnp.bfloat16


def repeat(low, high, step):
    if high - low <= 8:
        for k in range(low, high):
            step(k)
    else:

        def once(k, carry):
            step(k)
            return carry

        lax.fori_loop(low, high, once, 0)


def block(index, size):
    if isinstance(index, int):
        return pl.ds(index * size, size)
    return pl.ds(pl.multiple_of(index * size, size), size)


def partner(rank, k, size):
    assert size & (size - 1) == 0
    found, bit = 0, 1
    while bit < size:
        found = found + bit * ((rank // bit + k // bit) % 2)
        bit *= 2
    return found


def far_first(size, step):
    repeat(1, size, lambda m: step(size - m))


def dot(a, b):
    return jnp.dot(a, b, preferred_element_type=F32)


def gelu_and_slope(v):
    scale = 0.7978845608028654
    square = v * v
    t = jnp.tanh(scale * (v + 0.044715 * v * square))
    half = 0.5 * (1.0 + t)
    slope = half + 0.5 * v * (1.0 - t * t) * scale * (1.0 + 3 * 0.044715 * square)
    return v * half, slope


PARTS = 2


def kernel(
    n_row, n_col,
    feat_in, tiles_in, rows_ref, cols_ref, count_ref, weight_in, upstream_in,
    act, fgrad, wgrad,
    feat_all, tiles, tiles_t, adj, adj_t, weight, weight_t, upstream,
    part_send, part_recv, cot_all, sib_send, sib_recv, back_send, back_recv,
    w_send, w_recv, w_mid, w_all, slot_of,
    in_sem, sib_s, sib_r,
    feat_s, feat_r, fwd_s, fwd_r, part_s, part_r, cot_s, cot_r,
    pair_s, pair_r, back_s, back_r, w1_s, w1_r, w2_s, w2_r, w3_s, w3_r,
):
    i, j = lax.axis_index("row"), lax.axis_index("col")
    chip, core = i // 2, i % 2
    n_chip = n_row // 2
    sibling = 2 * chip + 1 - core
    nodes, width = feat_in.shape
    slots, tile = tiles_in.shape[0], tiles_in.shape[1]
    row_tiles = n_col * nodes // tile
    col_tiles = n_row * nodes // tile
    half = width // 2
    piece = 2 * width // n_row
    lanes = width // PARTS

    def to_row(src, dst, send, recv, peer):
        return pltpu.make_async_remote_copy(
            src_ref=src, dst_ref=dst, send_sem=send, recv_sem=recv,
            device_id=(peer, j), device_id_type=MESH)

    def to_col(src, dst, send, recv, peer):
        return pltpu.make_async_remote_copy(
            src_ref=src, dst_ref=dst, send_sem=send, recv_sem=recv,
            device_id=(i, peer), device_id_type=MESH)

    def row_peer(k):
        return partner(i, k, n_row)

    def col_peer(k):
        return partner(j, k, n_col)

    def mate(k):
        return 2 * partner(chip, k, n_chip) + core

    def strip(h):
        return pl.ds(h * lanes, lanes)

    loads = [
        pltpu.make_async_copy(tiles_in, tiles.at[pl.ds(0, slots)], in_sem.at[0]),
        pltpu.make_async_copy(weight_in, weight, in_sem.at[1]),
        pltpu.make_async_copy(upstream_in, upstream, in_sem.at[2]),
    ] + [
        pltpu.make_async_copy(feat_in.at[:, strip(h)], feat_all.at[h, block(i, nodes)],
                              in_sem.at[3 + h])
        for h in range(PARTS)
    ]
    for load in loads:
        load.start()

    barrier = pltpu.get_barrier_semaphore()
    repeat(1, n_row, lambda k: pl.semaphore_signal(
        barrier, inc=1, device_id=(row_peer(k), j), device_id_type=MESH))
    repeat(1, n_col, lambda k: pl.semaphore_signal(
        barrier, inc=1, device_id=(i, col_peer(k)), device_id_type=MESH))
    pl.semaphore_wait(barrier, n_row + n_col - 2)

    def feat_copy(h, k, owner):
        return to_row(feat_in.at[:, strip(h)], feat_all.at[h, block(owner, nodes)],
                      feat_s.at[h, k], feat_r.at[h, k], mate(k))

    def sib_copy(h, owner):
        return to_row(feat_in.at[:, strip(h)], feat_all.at[h, block(owner, nodes)],
                      sib_s.at[h], sib_r.at[h], sibling)

    def pass_copy(h, k, owner):
        place = feat_all.at[h, block(owner, nodes)]
        return to_row(place, place, fwd_s.at[h, k], fwd_r.at[h, k], sibling)

    for h in range(PARTS):
        far_first(n_chip, lambda k: feat_copy(h, k, i).start())
        sib_copy(h, i).start()

    count = count_ref[0, 0]
    places = [
        jnp.where(s < count, rows_ref[0, 0, s] * col_tiles + cols_ref[0, 0, s], -1)
        for s in range(slots)
    ]

    def find(spot):
        slot = jnp.int32(slots)
        for s, place in enumerate(places):
            slot = jnp.where(place == spot, jnp.int32(s), slot)
        slot_of[spot] = slot

    repeat(0, row_tiles, lambda r: repeat(0, col_tiles, lambda c: find(r * col_tiles + c)))
    tiles[slots] = jnp.zeros((tile, tile), BF16)
    tiles_t[slots] = jnp.zeros((tile, tile), BF16)
    loads[0].wait()

    def place_row(r):
        def place(c):
            adj[block(r, tile), block(c, tile)] = tiles[slot_of[r * col_tiles + c]]

        repeat(0, col_tiles, place)

    repeat(0, row_tiles, place_row)
    for load in loads[3:]:
        load.wait()

    last = PARTS - 1
    few = nodes // 2
    chunks = [(h, 0, nodes) for h in range(last)] + [(last, 0, few), (last, few, few)]

    def part_copy(n, k):
        h, first, size = chunks[n]
        rows = pl.ds(pl.multiple_of(col_peer(k) * nodes + first, few), size)
        return to_col(part_send.at[h, rows], part_recv.at[h, k, pl.ds(first, size)],
                      part_s.at[n, k], part_r.at[n, k], col_peer(k))

    for h in range(PARTS):

        def pass_on(k):
            feat_copy(h, k, mate(k)).wait_recv()
            pass_copy(h, k, mate(k)).start()

        far_first(n_chip, pass_on)
        sib_copy(h, sibling).wait_recv()
        far_first(n_chip, lambda k: pass_copy(h, k, mate(k) + sibling - i).wait_recv())

        part_send[h] = dot(adj[...], feat_all[h]).astype(BF16)
        for n, chunk in enumerate(chunks):
            if chunk[0] == h:
                far_first(n_col, lambda k: part_copy(n, k).start())
        part_recv[h, 0] = part_send[h, block(j, nodes), :]

    def flip(s):
        tiles_t[s] = tiles[s].T

    repeat(0, slots, flip)
    per = nodes // tile

    def place_back(r):
        def place(c):
            rank = c // per
            spot = ((rank % 2) * n_chip + rank // 2) * per + c % per
            adj_t[block(spot, tile), block(r, tile)] = tiles_t[slot_of[r * col_tiles + c]]

        repeat(0, col_tiles, place)

    repeat(0, row_tiles, place_back)
    loads[1].wait()
    loads[2].wait()
    weight_t[...] = weight[...].T
    for h in range(PARTS):

        def feat_sent(k):
            feat_copy(h, k, i).wait_send()
            pass_copy(h, k, mate(k)).wait_send()

        sib_copy(h, i).wait_send()
        repeat(1, n_chip, feat_sent)

    sendings = [(0, 0, few), (0, few, few)] + [(h, 0, nodes) for h in range(1, PARTS)]

    def cot_copy(n, k, owner):
        h, first, size = sendings[n]
        place = cot_all.at[h, pl.ds(pl.multiple_of(owner * nodes + first, few), size)]
        return to_col(place, place, cot_s.at[n, k], cot_r.at[n, k], col_peer(k))

    aggregates, cotangents = [], []
    for first in (0, few):
        rows = pl.ds(first, few)
        gathered = []
        preact = jnp.zeros((few, width), F32)
        for h in range(PARTS):
            for n, chunk in enumerate(chunks):
                if chunk[0] == h and (chunk[1] == first):
                    far_first(n_col, lambda k: part_copy(n, k).wait_recv())
            total = part_recv[h, 0, rows, :].astype(F32)
            for k in range(1, n_col):
                total = total + part_recv[h, k, rows, :].astype(F32)
            gathered.append(total.astype(BF16))
            preact = preact + dot(gathered[h], weight[strip(h), :])
        value, slope = gelu_and_slope(preact)
        cotangent = (upstream[rows, :].astype(F32) * slope).astype(BF16)
        for h in range(PARTS):
            spot = pl.ds(pl.multiple_of(j * nodes + first, few), few)
            cot_all[h, spot, :] = cotangent[:, h * lanes:(h + 1) * lanes]
        for n in range(len(sendings)):
            if (n == 0) == (first == 0):
                far_first(n_col, lambda k: cot_copy(n, k, j).start())
        act[rows, :] = value.astype(BF16)
        aggregates.append(jnp.concatenate(gathered, axis=1))
        cotangents.append(cotangent)
    aggregate = jnp.concatenate(aggregates, axis=0)
    cotangent = jnp.concatenate(cotangents, axis=0)

    term = lax.dot_general(aggregate, cotangent, (((0,), (0,)), ((), ())),
                           preferred_element_type=F32)
    term = (term * (nodes * n_row * n_col) ** -0.5).astype(BF16)
    w_send[pl.ds(0, width), :] = term[:, :half]
    w_send[pl.ds(width, width), :] = term[:, half:]

    def w1_copy(k):
        return to_row(w_send.at[block(row_peer(k), piece)], w_recv.at[k],
                      w1_s.at[k], w1_r.at[k], row_peer(k))

    far_first(n_row, lambda k: w1_copy(k).start())
    w_recv[0] = w_send[block(i, piece), :]
    for n in range(len(chunks)):
        repeat(1, n_col, lambda k: part_copy(n, k).wait_send())

    def w2_copy(k, owner):
        return to_col(w_mid.at[owner], w_mid.at[owner], w2_s.at[k], w2_r.at[k], col_peer(k))

    def w3_copy(k, owner):
        place = w_all.at[block(owner, piece)]
        return to_row(place, place, w3_s.at[k], w3_r.at[k], row_peer(k))

    def sum_over_row():
        far_first(n_row, lambda k: w1_copy(k).wait_recv())
        summed = w_recv[0].astype(F32)
        for k in range(1, n_row):
            summed = summed + w_recv[k].astype(F32)
        w_mid[j] = summed.astype(BF16)
        far_first(n_col, lambda k: w2_copy(k, j).start())

    def sum_over_col():
        far_first(n_col, lambda k: w2_copy(k, col_peer(k)).wait_recv())
        summed = w_mid[0].astype(F32)
        for k in range(1, n_col):
            summed = summed + w_mid[k].astype(F32)
        w_all[block(i, piece), :] = summed.astype(BF16)
        far_first(n_row, lambda k: w3_copy(k, i).start())

    def pair_copy(h):
        return to_row(sib_send.at[h], sib_recv.at[h], pair_s.at[h], pair_r.at[h], sibling)

    def back_copy(h, k):
        return to_row(back_send.at[h, block(partner(chip, k, n_chip), nodes)],
                      back_recv.at[h, k], back_s.at[h, k], back_r.at[h, k], mate(k))

    for h in range(PARTS):
        for n in (0, 1) if h == 0 else (h + 1,):
            far_first(n_col, lambda k: cot_copy(n, k, col_peer(k)).wait_recv())
        sib_send[h] = dot(adj_t[block(1 - core, n_chip * nodes), :], cot_all[h]).astype(BF16)
        pair_copy(h).start()
        mine = dot(adj_t[block(core, n_chip * nodes), :], cot_all[h])
        if h == 0:
            sum_over_row()
        if h == PARTS - 1:
            sum_over_col()
        pair_copy(h).wait_recv()
        back_send[h] = (mine + sib_recv[h].astype(F32)).astype(BF16)
        far_first(n_chip, lambda k: back_copy(h, k).start())
    for h in range(PARTS):
        pair_copy(h).wait_send()
    for n in range(len(sendings)):
        repeat(1, n_col, lambda k: cot_copy(n, k, j).wait_send())
    repeat(1, n_row, lambda k: w1_copy(k).wait_send())
    repeat(1, n_col, lambda k: w2_copy(k, j).wait_send())

    grad = jnp.zeros((nodes, width), F32)
    for h in range(PARTS):
        far_first(n_chip, lambda k: back_copy(h, k).wait_recv())
        pulled = back_send[h, block(chip, nodes), :].astype(F32)
        for k in range(1, n_chip):
            pulled = pulled + back_recv[h, k].astype(F32)
        grad = grad + dot(pulled.astype(BF16), weight_t[strip(h), :])
    fgrad[...] = grad.astype(BF16)

    far_first(n_row, lambda k: w3_copy(k, row_peer(k)).wait_recv())
    wgrad[:, pl.ds(0, half)] = w_all[pl.ds(0, width), :].astype(F32)
    wgrad[:, pl.ds(half, half)] = w_all[pl.ds(width, width), :].astype(F32)

    repeat(1, n_row, lambda k: w3_copy(k, i).wait_send())
    for h in range(PARTS):
        repeat(1, n_chip, lambda k: back_copy(h, k).wait_send())


def hand_over(*refs):
    sources, results, sems = refs[:3], refs[3:6], refs[6]
    copies = [
        pltpu.make_async_copy(source, result, sems.at[n])
        for n, (source, result) in enumerate(zip(sources, results))
    ]
    for copy in copies:
        copy.start()
    for copy in copies:
        copy.wait()


def body(features, tile_values, tile_rows, tile_cols, tile_count, weight, out_grad):
    n_row, n_col = lax.axis_size("row"), lax.axis_size("col")
    n_chip = n_row // 2
    nodes, width = features.shape
    slots, tile = tile_values.shape[2], tile_values.shape[3]
    tall, wide = n_col * nodes, n_row * nodes
    piece = 2 * width // n_row
    lanes = width // PARTS
    vmem, dma = pltpu.VMEM, pltpu.SemaphoreType.DMA
    anywhere = pl.BlockSpec(memory_space=pl.ANY)
    in_vmem = pl.BlockSpec(memory_space=pltpu.VMEM)
    scalars = pl.BlockSpec(memory_space=pltpu.SMEM)
    shapes = (
        jax.ShapeDtypeStruct((nodes, width), BF16),
        jax.ShapeDtypeStruct((nodes, width), BF16),
        jax.ShapeDtypeStruct((width, width), F32),
    )
    results = pl.pallas_call(
        functools.partial(kernel, n_row, n_col),
        out_shape=tuple(pltpu.VMEM(s.shape, s.dtype) for s in shapes),
        in_specs=[anywhere, anywhere, scalars, scalars, scalars, anywhere, anywhere],
        out_specs=(in_vmem,) * 3,
        scratch_shapes=[
            vmem((PARTS, wide, lanes), BF16),
            vmem((slots + 1, tile, tile), BF16),
            vmem((slots + 1, tile, tile), BF16),
            vmem((tall, wide), BF16),
            vmem((wide, tall), BF16),
            vmem((width, width), BF16),
            vmem((width, width), BF16),
            vmem((nodes, width), BF16),
            vmem((PARTS, tall, lanes), BF16),
            vmem((PARTS, n_col, nodes, lanes), BF16),
            vmem((PARTS, tall, lanes), BF16),
            vmem((PARTS, n_chip * nodes, lanes), BF16),
            vmem((PARTS, n_chip * nodes, lanes), BF16),
            vmem((PARTS, n_chip * nodes, lanes), BF16),
            vmem((PARTS, n_chip, nodes, lanes), BF16),
            vmem((2 * width, width // 2), BF16),
            vmem((n_row, piece, width // 2), BF16),
            vmem((n_col, piece, width // 2), BF16),
            vmem((2 * width, width // 2), BF16),
            pltpu.SMEM(((tall // tile) * (wide // tile),), jnp.int32),
            dma((3 + PARTS,)), dma((PARTS,)), dma((PARTS,)),
        ]
        + [dma((PARTS, n_chip))] * 4
        + [dma((PARTS + 1, n_col))] * 4
        + [dma((PARTS,))] * 2 + [dma((PARTS, n_chip))] * 2
        + [dma((n_row,))] * 2 + [dma((n_col,))] * 2 + [dma((n_row,))] * 2,
        compiler_params=pltpu.CompilerParams(
            collective_id=0, has_side_effects=True, vmem_limit_bytes=56 * 1024 * 1024),
    )(features, tile_values[0, 0], tile_rows, tile_cols, tile_count, weight, out_grad)
    return tuple(pl.pallas_call(
        hand_over,
        out_shape=shapes,
        in_specs=[in_vmem] * 3,
        out_specs=(anywhere,) * 3,
        scratch_shapes=[dma((3,))],
    )(*(pltpu.with_memory_space_constraint(r, pltpu.VMEM) for r in results)))


def solution(mesh):
    placed = (
        P(("row", "col"), None),
        P("row", "col", None, None, None),
        P("row", "col", None),
        P("row", "col", None),
        P("row", "col"),
        P(),
        P(("row", "col"), None),
    )
    return jax.shard_map(
        body,
        mesh=mesh,
        in_specs=placed,
        out_specs=(P(("row", "col"), None), P(("row", "col"), None), P()),
        check_vma=False,
    )
```
